256 devices in a mesh: dp: 16 (over x, z_hi), mp: 4 (over y), pre: 4 (over z_lo, core).
Axes of the slice: x: 4, y: 4, z: 8 (z_hi: 4, z_lo: 2; z = z_hi * 2 + z_lo), core: 2. Of those that a mesh axis runs over, the one named last changes fastest.
Arguments:
- activations: bfloat16 [4096, 16384], P('dp', 'mp'), may hold values from -12.7 to 12.7
- cotangent: bfloat16 [4096, 4096], P('dp', 'pre'), may hold values from -12.7 to 12.7
- weight_blocks: bfloat16 [16, 4, 4, 512, 512], P('dp', 'mp', 'pre'), may hold values from -0.09375 to 0.09375
- left_stat: float32 [16, 4, 4, 512, 512], P('dp', 'mp', 'pre'), may hold values from -0.01875 to 0.8625, as said below
- right_stat: float32 [16, 4, 4, 512, 512], P('dp', 'mp', 'pre'), may hold values from -0.01875 to 0.8625, as said below
Outputs:
- input_grad: bfloat16 [4096, 16384], P('dp', ('mp', 'pre'))
- left_next: float32 [16, 4, 4, 512, 512], P('dp', 'mp', 'pre')
- right_next: float32 [16, 4, 4, 512, 512], P('dp', 'mp', 'pre')
- update: float32 [16, 4, 4, 512, 512], P('dp', 'mp', 'pre')
The draws below stay inside these ranges and needn't reach their ends.
Inputs may be any that keep to these rules, and one draw needn't show every extreme that they name: `left_stat`: every block [k, m, p] is symmetric and positive definite. `right_stat`: every block [k, m, p] is symmetric and positive definite.
All inputs are finite; a program needn't handle non-finite values.
Results may differ from the reference program's by a relative error of at most 0.001.
Values may be sent and summed in bfloat16 or wider, within the bound.
A program may use at most 128 MiB of HBM per device.

```python
import math
import jax
import jax.numpy as jnp
from jax import lax

D = 4096
FF = 16384
BLOCK = 512
ITERS = 2
TOKENS = 4096
MP_PARTS = 4
PRE_PARTS = 4
ROW_TILES = 8
COL_TILES = 2
TILE_COUNT = 16


def scaled_columns(key, columns):
    scale_key, value_key = jax.random.split(key)
    scales = jnp.exp(jax.random.uniform(scale_key, (1, columns), jnp.float32, -1.15, 1.15))
    values = jnp.clip(jax.random.normal(value_key, (TOKENS, columns), jnp.float32), -4.0, 4.0)
    return (scales * values).astype(jnp.bfloat16)


def draw_activations(key, part):
    key = jax.random.fold_in(key, 11)
    return scaled_columns(key, FF)


def draw_cotangent(key, part):
    key = jax.random.fold_in(key, 12)
    return scaled_columns(key, D)


def stat_blocks(key):
    count = TILE_COUNT * MP_PARTS * PRE_PARTS
    band_key, diag_key, level_key = jax.random.split(key, 3)
    position = jnp.arange(count, dtype=jnp.float32) / max(count - 1, 1)
    level = jnp.exp(-math.log(9.0) * position) * jnp.exp(jax.random.uniform(level_key, (count,), jnp.float32, -0.35, 0.35))
    unit_scale = 0.1 * BLOCK / TOKENS * level[:, None, None]
    raw_band = jax.random.uniform(band_key, (count, BLOCK, BLOCK), jnp.float32, -1.0, 1.0)
    symmetric = 0.5 * (raw_band + jnp.swapaxes(raw_band, 1, 2))
    row_index = jnp.arange(BLOCK, dtype=jnp.int32)[:, None]
    col_index = jnp.arange(BLOCK, dtype=jnp.int32)[None, :]
    distance = jnp.abs(row_index - col_index)
    band_mask = ((distance > 0) & (distance <= 8)).astype(jnp.float32)
    identity_mask = (distance == 0).astype(jnp.float32)
    diagonal = 16.0 * (1.0 + jax.random.uniform(diag_key, (count, BLOCK), jnp.float32, 0.25, 2.0))
    matrix = unit_scale * (symmetric * band_mask + diagonal[:, :, None] * identity_mask)
    return matrix.reshape(TILE_COUNT, MP_PARTS, PRE_PARTS, BLOCK, BLOCK)


def draw_left_stat(key, part):
    key = jax.random.fold_in(key, 21)
    return stat_blocks(key)


def draw_right_stat(key, part):
    key = jax.random.fold_in(key, 22)
    return stat_blocks(key)


def block_scale(key, shape, pieces, smallest, top_value):
    gain = 1.0
    for dim, parts in pieces:
        heights = jax.random.uniform(jax.random.fold_in(jax.random.fold_in(key, 6), dim), (parts,), jnp.float32, smallest / len(pieces), top_value / len(pieces))
        gain = gain * jnp.repeat(jnp.exp(heights), shape[dim] // parts).reshape((-1,) + (1,) * (len(shape) - 1 - dim))
    return gain


def centred(key, dims, deviation, reach, cuts=(), held_as=jnp.bfloat16):
    level = block_scale(key, dims, cuts, -0.22, 0.18) if cuts else 1.0
    values = jax.random.normal(key, dims, jnp.float32) * deviation * level
    return jnp.minimum(jnp.maximum(values, -reach), reach).astype(held_as)


def setup_inputs(seed: int = 0) -> dict:
    splits = jax.random.split(jax.random.key(seed), 6)
    return {
        "activations": draw_activations(jax.random.fold_in(splits[5], 71), 0),
        "cotangent": draw_cotangent(jax.random.fold_in(splits[5], 71), 0),
        "weight_blocks": centred(splits[2], (TILE_COUNT, MP_PARTS, PRE_PARTS, BLOCK, BLOCK), D ** -0.5, 0.09375, ((0, 16), (1, 4), (2, 4))),
        "left_stat": draw_left_stat(jax.random.fold_in(splits[5], 71), 0),
        "right_stat": draw_right_stat(jax.random.fold_in(splits[5], 71), 0),
    }


DECAY_RATE = 0.9
EXACT_PRECISION = lax.Precision.HIGHEST

def product(former, latter):
    return jnp.dot(former, latter, precision=EXACT_PRECISION, preferred_element_type=jnp.float32)

def inverse_root(statistic):
    identity = jnp.eye(BLOCK, dtype=jnp.float32)
    frobenius = jnp.sqrt(jnp.sum(statistic * statistic))
    scaling = 2.5 / frobenius
    matrix = scaling * statistic
    factor = (5.0 * identity - matrix) / 4.0
    root_now = scaling ** 0.25 * factor
    for turn_index in range(ITERS - 1):
        square = product(factor, factor)
        matrix = product(product(square, square), matrix)
        factor = (5.0 * identity - matrix) / 4.0
        root_now = product(root_now, factor)
    return root_now

def block_update(blocks):
    grad_block, left_old, right_old = blocks
    left_next = DECAY_RATE * left_old + (1.0 - DECAY_RATE) * product(grad_block, grad_block.T)
    right_next = DECAY_RATE * right_old + (1.0 - DECAY_RATE) * product(grad_block.T, grad_block)
    raw_update = product(product(inverse_root(left_next), grad_block), inverse_root(right_next))
    return (left_next, right_next, raw_update)

def reference(activations, cotangent, weight_blocks, left_stat, right_stat):
    gradient = jnp.dot(activations.T, cotangent, preferred_element_type=jnp.float32) / TOKENS
    grad_blocks = gradient.reshape(MP_PARTS, ROW_TILES, BLOCK, PRE_PARTS, COL_TILES, BLOCK)
    grad_blocks = grad_blocks.transpose(1, 4, 0, 3, 2, 5).reshape(TILE_COUNT * MP_PARTS * PRE_PARTS, BLOCK, BLOCK)
    weight_full = weight_blocks.reshape(ROW_TILES, COL_TILES, MP_PARTS, PRE_PARTS, BLOCK, BLOCK)
    weight_full = weight_full.transpose(2, 0, 4, 3, 1, 5).reshape(FF, D)
    input_grad = jnp.dot(cotangent, weight_full.T, preferred_element_type=jnp.float32).astype(jnp.bfloat16)
    left_flat = left_stat.reshape(-1, BLOCK, BLOCK)
    right_flat = right_stat.reshape(-1, BLOCK, BLOCK)
    left_next, right_next, raw_update = lax.map(block_update, (grad_blocks, left_flat, right_flat))
    mean_square = jnp.sum(raw_update * raw_update) / (FF * D)
    update = raw_update / jnp.sqrt(mean_square + 1e-06)
    shape_out = left_stat.shape
    return (input_grad, left_next.reshape(shape_out), right_next.reshape(shape_out), update.reshape(shape_out))
```

```python
import jax
import jax.numpy as jnp
from jax import lax
from jax.experimental import pallas as pl
from jax.experimental.pallas import tpu as pltpu
from jax.sharding import PartitionSpec as P

D = 4096
FF = 16384
TOKENS = 4096
BLOCK = 512
NX, NY, NZ = 4, 4, 8

DECAY_RATE = 0.9
MESH = pl.DeviceIdType.MESH
DMA = pltpu.SemaphoreType.DMA
HIGH = lax.Precision.HIGH


def gather_kernel(
    act, cot, wblk,
    ig_out, grad_out,
    ACT, OUTB, COT, CIG, WB, ACC, OB,
    loc_sem, a1_s, a1_r, a1o_s, a1o_r, tz_s, tz_r, sw_s, sw_r,
    b1_s, b1_r, ring_s, ring_r, c1_s, c1_r, w_s, w_r, ws_s, ws_r, o_s, o_r,
):
    dp = lax.axis_index("dp")
    y = lax.axis_index("mp")
    pre = lax.axis_index("pre")
    x = lax.div(dp, 4)
    zh = lax.rem(dp, 4)
    zl = lax.div(pre, 2)
    c = lax.rem(pre, 2)
    oc = 1 - c
    z = zh * 2 + zl
    grp = lax.div(z, 4)
    g = lax.rem(z, 4)
    side = lax.div(g, 2)
    inner = lax.rem(lax.div(g + 1, 2), 2)
    d = 1 - 2 * side
    so, sn, sf, se = 1 + side, 3 * side, 2 - side, 3 - 3 * side
    hpar = lax.rem(zh, 2)

    def dev(xx, yy, zz, cc):
        return {
            "dp": xx * 4 + lax.div(zz, 2),
            "mp": yy,
            "pre": lax.rem(zz, 2) * 2 + cc,
        }

    def xp(k):
        return lax.rem(x + k + 4, 4)

    def yp(k):
        return lax.rem(y + k + 4, 4)

    def zp(k):
        return lax.rem(z + k + 8, 8)

    def zp_d(sign):
        return lax.rem(z + sign * d + 8, 8)

    other = dev(x, y, z, oc)

    barrier = pltpu.get_barrier_semaphore()
    count = 0

    def greet(device):
        pl.semaphore_signal(barrier, inc=1, device_id=device, device_id_type=MESH)

    for k in range(4):
        for m in range(4):
            if k or m:
                greet({"dp": xp(k) * 4 + zh, "mp": y, "pre": lax.rem(pre + m, 4)})
                count += 1
    for k in range(1, 4):
        greet(dev(x, yp(k), z, c))
        count += 1
    greet(dev(x, y, lax.rem(z + 2 * zl - 1 + 8, 8), c))
    greet(dev(x, y, zp(2), c))
    greet(dev(x, y, zp(-2), c))
    greet(dev(x, y, zp(4), c))
    count += 4
    pl.semaphore_wait(barrier, count)

    sends = []

    def remote(src, dst, ssem, rsem, device, when=None):
        cp = pltpu.make_async_remote_copy(
            src_ref=src, dst_ref=dst, send_sem=ssem, recv_sem=rsem,
            device_id=device, device_id_type=MESH,
        )
        if when is None:
            cp.start()
        else:
            @pl.when(when)
            def _():
                cp.start()
        sends.append((when, cp))

    def arrived(dst, rsem):
        pltpu.make_async_copy(dst, dst, rsem).wait()

    is_inner = inner == 1
    is_outer = inner == 0

    def act_src(xx, gg):
        return act.at[
            pl.ds(pl.multiple_of(c * 128, 128), 128),
            pl.ds(pl.multiple_of(xx * 1024 + gg * 512, 512), 512),
        ]

    rel = (0, -1, 1, 2)
    xs = [xp(r) for r in rel]
    cot_piece = lambda half: cot.at[
        pl.ds(pl.multiple_of(y * 64, 64), 64),
        pl.ds(pl.multiple_of(half * 512, 512), 512),
    ]
    ypair = lax.div(y, 2)
    ylow = lax.rem(y, 2)
    cot_slot = lambda zz: COT.at[zz, ypair, x, ylow]
    pltpu.make_async_copy(cot_piece(hpar), cot_slot(zh), loc_sem.at[0]).start()
    remote(cot_piece(hpar), cot_slot(zh), b1_s.at[0], b1_r.at[0], dev(x, y, zp(4), c))
    remote(cot_piece(1 - hpar), cot_slot(zh), b1_s.at[1], b1_r.at[1], dev(x, y, zp(2), c))
    remote(cot_piece(1 - hpar), cot_slot(zh), b1_s.at[2], b1_r.at[2], dev(x, y, zp(-2), c))
    pltpu.make_async_copy(act_src(x, grp), ACT.at[so, c, x], loc_sem.at[1]).start()

    @pl.when(is_outer)
    def _():
        pltpu.make_async_copy(act_src(x, 1 - grp), OUTB.at[x], loc_sem.at[2]).start()

    for k, step in ((1, 1), (2, -1), (3, 2)):
        to = xp(step)
        remote(act_src(to, 1 - grp), OUTB.at[x], a1o_s.at[k], a1o_r.at[k],
               dev(to, y, z, c), when=is_outer)
        remote(act_src(to, grp), ACT.at[so, c, x], a1_s.at[k], a1_r.at[k], dev(to, y, z, c))
    cig_src = lambda q: cot.at[pl.ds(pl.multiple_of(q * 64, 64), 64), :]
    pltpu.make_async_copy(cig_src(pre), CIG.at[pre, x], loc_sem.at[3]).start()
    for k in range(1, 4):
        q = lax.rem(pre + k, 4)
        remote(cig_src(q), CIG.at[pre, x], c1_s.at[k], c1_r.at[k],
               {"dp": dp, "mp": y, "pre": q})
    pltpu.make_async_copy(wblk, WB.at[z, c], loc_sem.at[4]).start()
    remote(wblk, WB.at[z, c], ws_s.at[0], ws_r.at[0], other)

    def ring_start(base, unit, my, to_next, to_prev):
        remote(unit(my, 0, 2), unit(my, 0, 2), ring_s.at[base], ring_r.at[base], to_next)
        remote(unit(my, 0, 2), unit(my, 0, 2), ring_s.at[base + 1], ring_r.at[base + 1], to_prev)

    def ring_forward(base, unit, prv, nxt, to_next, to_prev):
        arrived(unit(prv, 0, 2), ring_r.at[base])
        remote(unit(prv, 0, 1), unit(prv, 0, 1), ring_s.at[base + 2], ring_r.at[base + 2], to_next)
        arrived(unit(nxt, 0, 2), ring_r.at[base + 1])
        remote(unit(nxt, 1, 1), unit(nxt, 1, 1), ring_s.at[base + 3], ring_r.at[base + 3], to_prev)

    def ring_end(base, unit, far):
        arrived(unit(far, 0, 1), ring_r.at[base + 2])
        arrived(unit(far, 1, 1), ring_r.at[base + 3])

    xnext, xprev = dev(xp(1), y, z, c), dev(xp(-1), y, z, c)
    ynext, yprev = dev(x, yp(1), z, c), dev(x, yp(-1), z, c)
    u1a = lambda i, lo, n: COT.at[pl.ds(lo, n), ypair, i, ylow]
    u2a = lambda i, lo, n: COT.at[pl.ds(2 + lo, n), lax.div(i, 2), x, lax.rem(i, 2)]
    u1b = lambda i, lo, n: COT.at[pl.ds(lo, n), lax.div(i, 2), :, lax.rem(i, 2)]
    u2b = lambda i, lo, n: COT.at[pl.ds(2 + lo, n), :, i]
    uc = lambda i, lo, n: CIG.at[pl.ds(2 * lo, 2 * n), i]
    xargs = (xp(-1), xp(1), xnext, xprev)
    yargs = (yp(-1), yp(1), ynext, yprev)

    inward = dev(x, y, zp_d(1), c)
    outward = dev(x, y, zp_d(-1), c)
    kind_n = 2 * inner

    def swap(kind, k, slot):
        piece = ACT.at[slot, c, xs[k]]
        remote(piece, piece, sw_s.at[kind, k], sw_r.at[kind, k], other)

    def own(k):
        piece = ACT.at[so, c, xs[k]]
        if k == 0:
            pltpu.make_async_copy(act_src(x, grp), piece, loc_sem.at[1]).wait()

            @pl.when(is_outer)
            def _():
                pltpu.make_async_copy(act_src(x, 1 - grp), OUTB.at[x], loc_sem.at[2]).wait()
        else:
            @pl.when(is_outer)
            def _():
                arrived(OUTB.at[xs[k]], a1o_r.at[k])

        remote(OUTB.at[xs[k]], ACT.at[3 - sn, c, xs[k]],
               tz_s.at[0, k], tz_r.at[0, k], outward, when=is_outer)
        if k:
            arrived(piece, a1_r.at[k])
        remote(piece, piece, tz_s.at[1, k], tz_r.at[1, k], inward, when=is_inner)
        swap(3, k, so)

    def near(k):
        piece = ACT.at[sn, c, xs[k]]
        arrived(piece, tz_r.at[0, k])
        remote(piece, piece, tz_s.at[2, k], tz_r.at[kind_n, k], inward)
        swap(0, k, sn)

    def far(k):
        piece = ACT.at[sf, c, xs[k]]
        arrived(piece, tz_r.at[1, k])
        remote(piece, piece, tz_s.at[3, k], tz_r.at[1, k], outward, when=is_inner)
        swap(1, k, sf)

    def end(k):
        piece = ACT.at[se, c, xs[k]]
        arrived(piece, tz_r.at[2, k])
        remote(piece, piece, tz_s.at[4, k], tz_r.at[2, k], outward, when=is_inner)
        swap(2, k, se)

    own(0)
    pltpu.make_async_copy(cot_piece(hpar), cot_slot(zh), loc_sem.at[0]).wait()
    arrived(cot_slot(lax.rem(zh + 2, 4)), b1_r.at[0])
    arrived(cot_slot(lax.rem(zh + 3, 4)), b1_r.at[1])
    arrived(cot_slot(lax.rem(zh + 1, 4)), b1_r.at[2])
    ring_start(0, u1a, x, xnext, xprev)
    ring_start(4, u2a, y, ynext, yprev)
    own(1)
    own(2)
    near(0)
    ring_forward(0, u1a, *xargs)
    ring_forward(4, u2a, *yargs)
    far(0)
    near(1)
    ring_end(0, u1a, xp(2))
    ring_end(4, u2a, yp(2))
    ring_start(8, u1b, y, ynext, yprev)
    ring_start(12, u2b, x, xnext, xprev)
    own(3)
    near(2)
    far(1)
    end(0)
    near(3)
    far(2)
    end(1)
    far(3)
    end(2)
    end(3)
    pltpu.make_async_copy(wblk, WB.at[z, c], loc_sem.at[4]).wait()
    znext, zprev = dev(x, y, zp(1), c), dev(x, y, zp(-1), c)
    wpart = lambda zz, hf: WB.at[zz, c, pl.ds(hf * 256, 256)]

    def w_send(way, t, hf):
        zz = zp(-(t - 1)) if way == 0 else zp(t - 1)
        remote(wpart(zz, hf), wpart(zz, hf), w_s.at[way, t, hf], w_r.at[way, t, hf],
               znext if way == 0 else zprev)

    for hf in range(2):
        for way in range(2):
            w_send(way, 1, hf)
    ring_forward(8, u1b, *yargs)
    ring_forward(12, u2b, *xargs)
    ring_end(8, u1b, yp(2))
    ring_end(12, u2b, xp(2))
    pltpu.make_async_copy(cig_src(pre), CIG.at[pre, x], loc_sem.at[3]).wait()
    for k in range(1, 4):
        arrived(CIG.at[lax.rem(pre + 4 - k, 4), x], c1_r.at[k])
    ring_start(16, uc, x, xnext, xprev)
    for kind, slot in ((3, so), (0, sn), (1, sf), (2, se)):
        for k in range(4):
            arrived(ACT.at[slot, oc, xs[k]], sw_r.at[kind, k])

    grad_out[...] = jnp.zeros((BLOCK, BLOCK), jnp.float32)

    @pl.loop(0, 8)
    def _(i):
        s = lax.div(i, 2)
        cc = lax.rem(i, 2)
        shard = lax.rem(2 * grp + 3 + s, 4)
        a = ACT[s, cc].reshape(BLOCK, BLOCK)
        b = COT[shard, cc].reshape(BLOCK, BLOCK)
        grad_out[...] += lax.dot_general(
            a, b, (((0,), (0,)), ((), ())), preferred_element_type=jnp.float32
        )

    grad_out[...] = grad_out[...] * (1.0 / TOKENS)

    ACC[...] = jnp.zeros_like(ACC)

    def w_swap(way, t, hf):
        zz = zp(-t) if way == 0 else zp(t)
        remote(wpart(zz, hf), wpart(zz, hf), ws_s.at[1 + (way * 5 + t) * 2 + hf],
               ws_r.at[1 + (way * 5 + t) * 2 + hf], other)

    def ig_part(zz, cc, r0, rows):
        p = lax.rem(zz, 2) * 2 + cc
        h = lax.rem(lax.div(zz, 2), 2)
        a = CIG[p, :, :, pl.ds(pl.multiple_of(h * 512, 512), 512)].reshape(256, 512)
        w = WB[zz, cc, pl.ds(r0, rows)]
        out = lax.dot_general(a, w, (((1,), (1,)), ((), ())), preferred_element_type=jnp.float32)
        ACC[lax.div(zz, 4), :, pl.ds(r0, rows)] += out

    def w_arrive(way, t, hf):
        zz = zp(-t) if way == 0 else zp(t)
        arrived(wpart(zz, hf), w_r.at[way, t, hf])
        if t < 3 or (t == 3 and hf == way):
            w_send(way, t + 1, hf)
        w_swap(way, t, hf)

    def other_half(way, t, hf):
        zz = zp(-t) if way == 0 else zp(t)
        arrived(WB.at[zz, oc, pl.ds(hf * 256, 256)], ws_r.at[1 + (way * 5 + t) * 2 + hf])

    ring_forward(16, uc, *xargs)
    for hf in range(2):
        for way in range(2):
            w_arrive(way, 1, hf)
    ring_end(16, uc, xp(2))
    arrived(WB.at[z, oc], ws_r.at[0])
    ig_part(z, c, 0, 512)
    ig_part(z, oc, 0, 512)
    for t in range(2, 5):
        for hf in range(2):
            for way in range(2):
                if t < 4 or hf == way:
                    w_arrive(way, t, hf)
        for way in range(2):
            zz = zp(-(t - 1)) if way == 0 else zp(t - 1)
            for hf in range(2):
                other_half(way, t - 1, hf)
            ig_part(zz, c, 0, 512)
            ig_part(zz, oc, 0, 512)
    z4 = zp(4)
    for way in range(2):
        other_half(way, 4, way)
    ig_part(z4, c, 0, 512)
    ig_part(z4, oc, 0, 512)

    for j in range(2):
        OB[:, :, pl.ds(j * 512, 512)] = ACC[j].reshape(4, 64, 512).astype(jnp.bfloat16)
    sub = zl * 2 + c
    z_to = zh * 2 + lax.div(x, 2)
    c_to = lax.rem(x, 2)
    rows = ig_out.at[pl.ds(pl.multiple_of(sub * 64, 64), 64), :]
    mine = pre == x
    for k in range(4):
        xt = xs[k]
        dst = dev(xt, y, z_to, c_to)
        if k == 0:
            remote(OB.at[xt], rows, o_s.at[k], o_r.at[sub], dst, when=jnp.logical_not(mine))

            @pl.when(mine)
            def _():
                cp = pltpu.make_async_copy(OB.at[x], rows, loc_sem.at[5])
                cp.start()
                cp.wait()
        else:
            remote(OB.at[xt], rows, o_s.at[k], o_r.at[sub], dst)
    for q in range(4):
        piece = ig_out.at[pl.ds(q * 64, 64), :]

        @pl.when(jnp.logical_not(jnp.logical_and(mine, sub == q)))
        def _():
            arrived(piece, o_r.at[q])

    for when, cp in sends:
        if when is None:
            cp.wait_send()
        else:
            pl.when(when)(cp.wait_send)


def gather_call(act, cot, wblk):
    any_spec = pl.BlockSpec(memory_space=pl.ANY)
    vmem = pl.BlockSpec(memory_space=pltpu.VMEM)
    bf = jnp.bfloat16
    return pl.pallas_call(
        gather_kernel,
        out_shape=(
            jax.ShapeDtypeStruct((256, 1024), bf),
            jax.ShapeDtypeStruct((BLOCK, BLOCK), jnp.float32),
        ),
        in_specs=[any_spec] * 3,
        out_specs=(any_spec, vmem),
        scratch_shapes=[
            pltpu.VMEM((4, 2, 4, 128, 512), bf),
            pltpu.VMEM((4, 128, 512), bf),
            pltpu.VMEM((4, 2, 4, 2, 64, 512), bf),
            pltpu.VMEM((4, 4, 64, 1024), bf),
            pltpu.VMEM((8, 2, 512, 512), bf),
            pltpu.VMEM((2, 256, 512), jnp.float32),
            pltpu.VMEM((4, 64, 1024), bf),
            DMA((6,)), DMA((4,)), DMA((4,)), DMA((4,)), DMA((4,)),
            DMA((5, 4)), DMA((3, 4)), DMA((4, 4)), DMA((4, 4)),
            DMA((3,)), DMA((3,)), DMA((20,)), DMA((20,)), DMA((4,)), DMA((4,)),
            DMA((2, 5, 2)), DMA((2, 5, 2)), DMA((21,)), DMA((21,)), DMA((4,)), DMA((4,)),
        ],
        compiler_params=pltpu.CompilerParams(
            collective_id=0, has_side_effects=True, vmem_limit_bytes=48 * 1024 * 1024
        ),
        name="gather_products",
    )(act, cot, wblk)


def product(former, latter):
    return jnp.dot(former, latter, precision=HIGH, preferred_element_type=jnp.float32)


def inverse_root(statistic):
    identity = jnp.eye(BLOCK, dtype=jnp.float32)
    frobenius = jnp.sqrt(jnp.sum(statistic * statistic))
    scaling = 2.5 / frobenius
    matrix = scaling * statistic
    factor = (5.0 * identity - matrix) / 4.0
    square = product(factor, factor)
    matrix = product(product(square, square), matrix)
    later = (5.0 * identity - matrix) / 4.0
    return product(scaling**0.25 * factor, later)


def on_device(activations, cotangent, weight_blocks, left_stat, right_stat):
    input_grad, grad = gather_call(
        activations, cotangent, weight_blocks.reshape(BLOCK, BLOCK)
    )
    left_old = left_stat.reshape(BLOCK, BLOCK)
    right_old = right_stat.reshape(BLOCK, BLOCK)
    left_next = DECAY_RATE * left_old + (1.0 - DECAY_RATE) * product(grad, grad.T)
    right_next = DECAY_RATE * right_old + (1.0 - DECAY_RATE) * product(grad.T, grad)
    raw_update = product(product(inverse_root(left_next), grad), inverse_root(right_next))
    square_sum = lax.psum(jnp.sum(raw_update * raw_update), ("dp", "mp", "pre"))
    update = raw_update / jnp.sqrt(square_sum / (FF * D) + 1e-06)
    shape_out = left_stat.shape
    return (
        input_grad,
        left_next.reshape(shape_out),
        right_next.reshape(shape_out),
        update.reshape(shape_out),
    )


def solution(mesh):
    block = P("dp", "mp", "pre", None, None)
    return jax.shard_map(
        on_device,
        mesh=mesh,
        in_specs=(P("dp", "mp"), P("dp", "pre"), block, block, block),
        out_specs=(P("dp", ("mp", "pre")), block, block, block),
        check_vma=False,
    )
```

```python
import jax
import jax.numpy as jnp
from jax import lax
from jax.experimental import pallas as pl
from jax.experimental.pallas import tpu as pltpu
from jax.sharding import PartitionSpec as P

D = 4096
FF = 16384
TOKENS = 4096
BLOCK = 512
NX, NY, NZ = 4, 4, 8

DECAY_RATE = 0.9
MESH = pl.DeviceIdType.MESH
DMA = pltpu.SemaphoreType.DMA
C0, C1, C2, C3 = 25 / 16, -(5 + 3125 / 256) / 16, 3125 / 4096, -1250 / 4096
C4, C5, C6 = 250 / 4096, -25 / 4096, 1 / 4096


def split(value):
    high = value.astype(jnp.bfloat16)
    return high, (value - high.astype(jnp.float32)).astype(jnp.bfloat16)


NN = (((1,), (0,)), ((), ()))
NT = (((1,), (1,)), ((), ()))
TN = (((0,), (0,)), ((), ()))


def dot(a, b, dims):
    return lax.dot_general(a, b, dims, preferred_element_type=jnp.float32)


def product(a, b, dims=NN):
    ah, al = a
    bh, bl = b
    return dot(ah, bh, dims) + (dot(ah, bl, dims) + dot(al, bh, dims))


def whole_kernel(
    act, cot, wblk, lstat, rstat,
    ig_out, left_out, right_out, update_out,
    ACT, OUTB, COT, CIG, WB, ACC, OB, G, GS, STAT, T2, T3, MS, CS, PS, RAW, RED,
    loc_sem, a1_s, a1_r, a1o_s, a1o_r, tz_s, tz_r, sw_s, sw_r,
    b1_s, b1_r, pa_s, pa_r, ring_s, ring_r, c1_s, c1_r, w_s, w_r, ws_s, ws_r, o_s, o_r,
    red_s, red_r, st_sem,
):
    dp = lax.axis_index("dp")
    y = lax.axis_index("mp")
    pre = lax.axis_index("pre")
    x = lax.div(dp, 4)
    zh = lax.rem(dp, 4)
    zl = lax.div(pre, 2)
    c = lax.rem(pre, 2)
    oc = 1 - c
    z = zh * 2 + zl
    grp = lax.div(z, 4)
    g = lax.rem(z, 4)
    side = lax.div(g, 2)
    inner = lax.rem(lax.div(g + 1, 2), 2)
    d = 1 - 2 * side
    so, sn, sf, se = 1 + side, 3 * side, 2 - side, 3 - 3 * side
    hpar = lax.rem(zh, 2)

    def dev(xx, yy, zz, cc):
        return {
            "dp": xx * 4 + lax.div(zz, 2),
            "mp": yy,
            "pre": lax.rem(zz, 2) * 2 + cc,
        }

    def xp(k):
        return lax.rem(x + k + 4, 4)

    def yp(k):
        return lax.rem(y + k + 4, 4)

    def zp(k):
        return lax.rem(z + k + 8, 8)

    def zp_d(sign):
        return lax.rem(z + sign * d + 8, 8)

    other = dev(x, y, z, oc)

    barrier = pltpu.get_barrier_semaphore()
    count = 0

    def greet(device):
        pl.semaphore_signal(barrier, inc=1, device_id=device, device_id_type=MESH)

    for k in range(4):
        for m in range(4):
            if k or m:
                greet({"dp": xp(k) * 4 + zh, "mp": y, "pre": lax.rem(pre + m, 4)})
                count += 1
    for k in range(1, 4):
        greet(dev(x, yp(k), z, c))
        count += 1
    pair = lax.rem(z + 1 - 2 * zl + 8, 8)
    for k in range(1, 7):
        greet(dev(x, y, lax.rem(pair + (1 - 2 * zl) * k + 16, 8), c))
        count += 1
    pl.semaphore_wait(barrier, count)

    sends = []

    def remote(src, dst, ssem, rsem, device, when=None):
        cp = pltpu.make_async_remote_copy(
            src_ref=src, dst_ref=dst, send_sem=ssem, recv_sem=rsem,
            device_id=device, device_id_type=MESH,
        )
        if when is None:
            cp.start()
        else:
            @pl.when(when)
            def _():
                cp.start()
        sends.append((when, cp))

    def arrived(dst, rsem):
        pltpu.make_async_copy(dst, dst, rsem).wait()

    is_inner = inner == 1
    is_outer = inner == 0

    def act_src(xx, gg):
        return act.at[
            pl.ds(pl.multiple_of(c * 128, 128), 128),
            pl.ds(pl.multiple_of(xx * 1024 + gg * 512, 512), 512),
        ]

    rel = (0, -1, 1, 2)
    xs = [xp(r) for r in rel]
    cot_piece = lambda half: cot.at[
        pl.ds(pl.multiple_of(y * 64, 64), 64),
        pl.ds(pl.multiple_of(half * 512, 512), 512),
    ]
    ypair = lax.div(y, 2)
    ylow = lax.rem(y, 2)
    cot_slot = lambda zz: COT.at[zz, ypair, x, ylow]
    pltpu.make_async_copy(cot_piece(hpar), cot_slot(zh), loc_sem.at[0]).start()
    remote(cot_piece(hpar), cot_slot(zh), b1_s.at[0], b1_r.at[0], dev(x, y, zp(4), c))
    remote(cot_piece(1 - hpar), cot_slot(zh), b1_s.at[1], b1_r.at[1], dev(x, y, zp(2), c))
    remote(cot_piece(1 - hpar), cot_slot(zh), b1_s.at[2], b1_r.at[2], dev(x, y, zp(-2), c))
    pltpu.make_async_copy(act_src(x, grp), ACT.at[so, c, x], loc_sem.at[1]).start()

    @pl.when(is_outer)
    def _():
        pltpu.make_async_copy(act_src(x, 1 - grp), OUTB.at[x], loc_sem.at[2]).start()

    for k, step in ((1, 1), (2, -1), (3, 2)):
        to = xp(step)
        remote(act_src(to, 1 - grp), OUTB.at[x], a1o_s.at[k], a1o_r.at[k],
               dev(to, y, z, c), when=is_outer)
        remote(act_src(to, grp), ACT.at[so, c, x], a1_s.at[k], a1_r.at[k], dev(to, y, z, c))
    cig_src = lambda q: cot.at[pl.ds(pl.multiple_of(q * 64, 64), 64), :]
    pltpu.make_async_copy(cig_src(pre), CIG.at[pre, x], loc_sem.at[3]).start()
    for k in range(1, 4):
        q = lax.rem(pre + k, 4)
        remote(cig_src(q), CIG.at[pre, x], c1_s.at[k], c1_r.at[k],
               {"dp": dp, "mp": y, "pre": q})
    pltpu.make_async_copy(wblk, WB.at[z, c], loc_sem.at[4]).start()
    remote(wblk, WB.at[z, c], ws_s.at[0], ws_r.at[0], other)

    def ring_start(base, unit, my, to_next, to_prev):
        for hf in range(2):
            remote(unit(my, hf), unit(my, hf), ring_s.at[base + hf], ring_r.at[base + hf], to_next)
            back = 1 - hf
            remote(unit(my, back), unit(my, back), ring_s.at[base + 2 + back],
                   ring_r.at[base + 2 + back], to_prev)

    def ring_forward(base, unit, prv, nxt, to_next, to_prev):
        arrived(unit(prv, 0), ring_r.at[base])
        remote(unit(prv, 0), unit(prv, 0), ring_s.at[base + 4], ring_r.at[base + 4], to_next)
        arrived(unit(nxt, 1), ring_r.at[base + 3])
        remote(unit(nxt, 1), unit(nxt, 1), ring_s.at[base + 5], ring_r.at[base + 5], to_prev)

    def ring_end(base, unit, prv, nxt, far):
        arrived(unit(prv, 1), ring_r.at[base + 1])
        arrived(unit(nxt, 0), ring_r.at[base + 2])
        arrived(unit(far, 0), ring_r.at[base + 4])
        arrived(unit(far, 1), ring_r.at[base + 5])

    xnext, xprev = dev(xp(1), y, z, c), dev(xp(-1), y, z, c)
    ynext, yprev = dev(x, yp(1), z, c), dev(x, yp(-1), z, c)
    u1a = lambda i: COT.at[pl.ds(0, 2), ypair, i, ylow]
    u2a = lambda i: COT.at[pl.ds(2, 2), lax.div(i, 2), x, lax.rem(i, 2)]
    u1b = lambda i, lo: COT.at[lo, lax.div(i, 2), :, lax.rem(i, 2)]
    u2b = lambda i, lo: COT.at[2 + lo, :, i]
    uc = lambda i, lo: CIG.at[pl.ds(2 * lo, 2), i]
    xargs = (xp(-1), xp(1), xnext, xprev)
    yargs = (yp(-1), yp(1), ynext, yprev)

    def cot_along_z():
        pltpu.make_async_copy(cot_piece(hpar), cot_slot(zh), loc_sem.at[0]).wait()
        arrived(cot_slot(lax.rem(zh + 3, 4)), b1_r.at[1])
        arrived(cot_slot(lax.rem(zh + 1, 4)), b1_r.at[2])
        arrived(cot_slot(lax.rem(zh + 2, 4)), b1_r.at[0])
        for k in (2, 1, 3):
            remote(u1a(x), u1a(x), pa_s.at[0, k], pa_r.at[0, k], dev(xp(k), y, z, c))
            remote(u2a(y), u2a(y), pa_s.at[1, k], pa_r.at[1, k], dev(x, yp(k), z, c))

    def cot_first():
        for k in (1, 3, 2):
            arrived(u1a(xp(-k)), pa_r.at[0, k])
            arrived(u2a(yp(-k)), pa_r.at[1, k])
        ring_start(0, u1b, y, ynext, yprev)
        ring_start(6, u2b, x, xnext, xprev)

    def cot_forward():
        ring_forward(0, u1b, *yargs)
        ring_forward(6, u2b, *xargs)

    def cot_end():
        ring_end(0, u1b, yp(-1), yp(1), yp(2))
        ring_end(6, u2b, xp(-1), xp(1), xp(2))

    def cig_first():
        pltpu.make_async_copy(cig_src(pre), CIG.at[pre, x], loc_sem.at[3]).wait()
        for k in range(1, 4):
            arrived(CIG.at[lax.rem(pre + 4 - k, 4), x], c1_r.at[k])
        ring_start(12, uc, x, xnext, xprev)

    def cig_forward():
        ring_forward(12, uc, *xargs)

    def cig_end():
        ring_end(12, uc, xp(-1), xp(1), xp(2))

    inward = dev(x, y, zp_d(1), c)
    outward = dev(x, y, zp_d(-1), c)
    kind_n = 2 * inner

    def swap(kind, k, slot):
        piece = ACT.at[slot, c, xs[k]]
        remote(piece, piece, sw_s.at[kind, k], sw_r.at[kind, k], other)

    def own(k):
        piece = ACT.at[so, c, xs[k]]
        if k == 0:
            pltpu.make_async_copy(act_src(x, grp), piece, loc_sem.at[1]).wait()

            @pl.when(is_outer)
            def _():
                pltpu.make_async_copy(act_src(x, 1 - grp), OUTB.at[x], loc_sem.at[2]).wait()
        else:
            @pl.when(is_outer)
            def _():
                arrived(OUTB.at[xs[k]], a1o_r.at[k])

        remote(OUTB.at[xs[k]], ACT.at[3 - sn, c, xs[k]],
               tz_s.at[0, k], tz_r.at[0, k], outward, when=is_outer)
        if k:
            arrived(piece, a1_r.at[k])
        remote(piece, piece, tz_s.at[1, k], tz_r.at[1, k], inward, when=is_inner)
        swap(3, k, so)

    def near(k):
        piece = ACT.at[sn, c, xs[k]]
        arrived(piece, tz_r.at[0, k])
        remote(piece, piece, tz_s.at[2, k], tz_r.at[kind_n, k], inward)
        swap(0, k, sn)

    def far(k):
        piece = ACT.at[sf, c, xs[k]]
        arrived(piece, tz_r.at[1, k])
        remote(piece, piece, tz_s.at[3, k], tz_r.at[1, k], outward, when=is_inner)
        swap(1, k, sf)

    def end(k):
        piece = ACT.at[se, c, xs[k]]
        arrived(piece, tz_r.at[2, k])
        remote(piece, piece, tz_s.at[4, k], tz_r.at[2, k], outward, when=is_inner)
        swap(2, k, se)

    znext, zprev = dev(x, y, zp(1), c), dev(x, y, zp(-1), c)
    wpart = lambda zz, hf: WB.at[zz, c, pl.ds(hf * 256, 256)]

    def w_send(way, t, hf):
        zz = zp(-(t - 1)) if way == 0 else zp(t - 1)
        remote(wblk.at[pl.ds(hf * 256, 256)] if t == 1 else wpart(zz, hf), wpart(zz, hf),
               w_s.at[way, t, hf], w_r.at[way, t, hf], znext if way == 0 else zprev)

    def w_index(way, t, hf):
        return 1 + (way * 5 + t) * 2 + hf

    def w_arrive(way, t, hf):
        zz = zp(-t) if way == 0 else zp(t)
        arrived(wpart(zz, hf), w_r.at[way, t, hf])
        if t < 3 or (t == 3 and hf == way):
            w_send(way, t + 1, hf)
        n = w_index(way, t, hf)
        remote(wpart(zz, hf), wpart(zz, hf), ws_s.at[n], ws_r.at[n], other)

    def w_first():
        for hf in range(2):
            for way in range(2):
                w_send(way, 1, hf)

    def w_step(t):
        for hf in range(2):
            for way in range(2):
                if t < 4 or hf == way:
                    w_arrive(way, t, hf)

    def ig_chip(zz):
        for cc in range(2):
            p = lax.rem(zz, 2) * 2 + cc
            h = lax.rem(lax.div(zz, 2), 2)
            a = CIG[p, :, :, pl.ds(pl.multiple_of(h * 512, 512), 512)].reshape(256, 512)
            ACC[lax.div(zz, 4)] += dot(a, WB[zz, cc], NT)

    def ig_own():
        pltpu.make_async_copy(wblk, WB.at[z, c], loc_sem.at[4]).wait()
        arrived(WB.at[z, oc], ws_r.at[0])
        ACC[...] = jnp.zeros_like(ACC)
        ig_chip(z)

    def ig_step(t):
        for way in range(2):
            zz = zp(-t) if way == 0 else zp(t)
            for hf in range(2):
                if t < 4 or hf == way:
                    arrived(WB.at[zz, oc, pl.ds(hf * 256, 256)], ws_r.at[w_index(way, t, hf)])
            if t < 4:
                ig_chip(zz)
        if t == 4:
            ig_chip(zp(4))

    def gradient():
        for kind, slot in ((3, so), (0, sn), (1, sf), (2, se)):
            for k in range(4):
                arrived(ACT.at[slot, oc, xs[k]], sw_r.at[kind, k])
        G[...] = jnp.zeros_like(G)

        @pl.loop(0, 8)
        def _(i):
            s = lax.div(i, 2)
            cc = lax.rem(i, 2)
            shard = lax.rem(2 * grp + 3 + s, 4)
            a = ACT[s, cc].reshape(BLOCK, BLOCK)
            b = COT[shard, cc].reshape(BLOCK, BLOCK)
            G[...] += dot(a, b, TN)

        grad = G[...] * (1.0 / TOKENS)
        high, low = split(grad)
        GS[0] = high
        GS[1] = low

    pair_of = lambda ref: (ref[0], ref[1])

    def put(ref, value):
        high, low = split(value)
        ref[0] = high
        ref[1] = low

    def statistic(i, dims, old, new):
        pltpu.make_async_copy(old, STAT.at[i], st_sem.at[i]).wait()
        g = pair_of(GS)
        STAT[i] = DECAY_RATE * STAT[i] + (1.0 - DECAY_RATE) * product(g, g, dims)
        cp = pltpu.make_async_copy(STAT.at[i], new, st_sem.at[2 + i])
        cp.start()
        local_out.append(cp)

    scale = [None, None]

    def root_1(i):
        a = STAT[i]
        z_of = 2.5 * lax.rsqrt(jnp.sum(a * a, axis=(0, 1), keepdims=True))
        scale[i] = z_of
        put(MS, z_of * a)
        T2[...] = product(pair_of(MS), pair_of(MS))
        put(CS, T2[...])

    def root_2(i):
        T3[...] = product(pair_of(MS), pair_of(CS))

    def root_3(i):
        m = scale[i] * STAT[i]
        put(CS, C4 * m + C5 * T2[...] + C6 * T3[...])
        put(MS, T3[...])
        eye = (
            lax.broadcasted_iota(jnp.int32, (BLOCK, BLOCK), 0)
            == lax.broadcasted_iota(jnp.int32, (BLOCK, BLOCK), 1)
        )
        low_part = C1 * m + C2 * T2[...] + C3 * T3[...] + jnp.where(eye, C0, 0.0)
        whole = low_part + product(pair_of(MS), pair_of(CS))
        put(PS.at[i], jnp.sqrt(jnp.sqrt(scale[i])) * whole)

    def raw_1():
        put(CS, product(pair_of(PS.at[0]), pair_of(GS)))

    def raw_2():
        raw = product(pair_of(CS), pair_of(PS.at[1]))
        RAW[...] = raw
        RED[0] = jnp.broadcast_to(jnp.sum(raw * raw, axis=(0, 1), keepdims=True), (8, 128))

    def red_targets(stage):
        if stage == 0:
            return [(1, other)]
        if stage == 1:
            return [(1 + k, dev(x, y, zp(k), c)) for k in range(1, 8)]
        if stage == 2:
            return [(8 + k, dev(xp(k), y, z, c)) for k in range(1, 4)]
        return [(11 + k, dev(x, yp(k), z, c)) for k in range(1, 4)]

    def red_send(stage):
        for slot, device in red_targets(stage):
            remote(RED.at[15 + stage], RED.at[slot], red_s.at[slot], red_r.at[slot], device)

    def red_start(stage):
        RED[15 + stage] = RED[0]
        red_send(stage)

    def red_finish(stage):
        total = RED[0]
        for slot, _ in red_targets(stage):
            arrived(RED.at[slot], red_r.at[slot])
            total = total + RED[slot]
        RED[0] = total

    def update():
        mean_square = RED[0, 0:1, 0:1] * (1.0 / (FF * D))
        RAW[...] = RAW[...] * lax.rsqrt(mean_square + 1e-06)
        cp = pltpu.make_async_copy(RAW, update_out, st_sem.at[4])
        cp.start()
        local_out.append(cp)

    local_out = []
    pltpu.make_async_copy(lstat, STAT.at[0], st_sem.at[0]).start()
    pltpu.make_async_copy(rstat, STAT.at[1], st_sem.at[1]).start()

    own(0)
    w_first()
    cot_along_z()
    own(1)
    own(2)
    near(0)
    cot_first()
    far(0)
    near(1)
    own(3)
    near(2)
    far(1)
    end(0)
    cot_forward()
    w_step(1)
    near(3)
    far(2)
    end(1)
    cig_first()
    far(3)
    end(2)
    end(3)
    cot_end()
    w_step(2)
    cig_forward()
    gradient()
    statistic(0, NT, lstat, left_out)
    statistic(1, TN, rstat, right_out)
    root_1(0)
    root_2(0)
    w_step(3)
    root_3(0)
    root_1(1)
    root_2(1)
    root_3(1)
    raw_1()
    raw_2()
    red_start(0)
    cig_end()
    red_finish(0)
    red_start(1)
    ig_own()
    ig_step(1)
    red_finish(1)
    red_start(2)
    ig_step(2)
    red_finish(2)
    red_start(3)
    ig_step(3)
    red_finish(3)
    update()
    w_step(4)
    ig_step(4)

    for j in range(2):
        OB[:, :, pl.ds(j * 512, 512)] = ACC[j].reshape(4, 64, 512).astype(jnp.bfloat16)
    sub = zl * 2 + c
    z_to = zh * 2 + lax.div(x, 2)
    c_to = lax.rem(x, 2)
    rows = ig_out.at[pl.ds(pl.multiple_of(sub * 64, 64), 64), :]
    mine = pre == x
    for k in range(4):
        xt = xs[k]
        dst = dev(xt, y, z_to, c_to)
        if k == 0:
            remote(OB.at[xt], rows, o_s.at[k], o_r.at[sub], dst, when=jnp.logical_not(mine))

            @pl.when(mine)
            def _():
                cp = pltpu.make_async_copy(OB.at[x], rows, loc_sem.at[5])
                cp.start()
                cp.wait()
        else:
            remote(OB.at[xt], rows, o_s.at[k], o_r.at[sub], dst)
    for q in range(4):
        piece = ig_out.at[pl.ds(q * 64, 64), :]

        @pl.when(jnp.logical_not(jnp.logical_and(mine, sub == q)))
        def _():
            arrived(piece, o_r.at[q])

    for cp in local_out:
        cp.wait()
    for when, cp in sends:
        if when is None:
            cp.wait_send()
        else:
            pl.when(when)(cp.wait_send)


def whole_call(act, cot, wblk, lstat, rstat):
    any_spec = pl.BlockSpec(memory_space=pl.ANY)
    bf, f32 = jnp.bfloat16, jnp.float32
    square = jax.ShapeDtypeStruct((BLOCK, BLOCK), f32)
    return pl.pallas_call(
        whole_kernel,
        out_shape=(jax.ShapeDtypeStruct((256, 1024), bf), square, square, square),
        in_specs=[any_spec] * 5,
        out_specs=(any_spec,) * 4,
        scratch_shapes=[
            pltpu.VMEM((4, 2, 4, 128, 512), bf),
            pltpu.VMEM((4, 128, 512), bf),
            pltpu.VMEM((4, 2, 4, 2, 64, 512), bf),
            pltpu.VMEM((4, 4, 64, 1024), bf),
            pltpu.VMEM((8, 2, 512, 512), bf),
            pltpu.VMEM((2, 256, 512), f32),
            pltpu.VMEM((4, 64, 1024), bf),
            pltpu.VMEM((BLOCK, BLOCK), f32),
            pltpu.VMEM((2, BLOCK, BLOCK), bf),
            pltpu.VMEM((2, BLOCK, BLOCK), f32),
            pltpu.VMEM((BLOCK, BLOCK), f32),
            pltpu.VMEM((BLOCK, BLOCK), f32),
            pltpu.VMEM((2, BLOCK, BLOCK), bf),
            pltpu.VMEM((2, BLOCK, BLOCK), bf),
            pltpu.VMEM((2, 2, BLOCK, BLOCK), bf),
            pltpu.VMEM((BLOCK, BLOCK), f32),
            pltpu.VMEM((19, 8, 128), f32),
            DMA((6,)), DMA((4,)), DMA((4,)), DMA((4,)), DMA((4,)),
            DMA((5, 4)), DMA((3, 4)), DMA((4, 4)), DMA((4, 4)),
            DMA((3,)), DMA((3,)), DMA((2, 4)), DMA((2, 4)), DMA((18,)), DMA((18,)),
            DMA((4,)), DMA((4,)), DMA((2, 5, 2)), DMA((2, 5, 2)), DMA((21,)), DMA((21,)),
            DMA((4,)), DMA((4,)), DMA((15,)), DMA((15,)), DMA((5,)),
        ],
        compiler_params=pltpu.CompilerParams(
            collective_id=0, has_side_effects=True, vmem_limit_bytes=60 * 1024 * 1024
        ),
        name="gather_products",
    )(act, cot, wblk, lstat, rstat)


def on_device(activations, cotangent, weight_blocks, left_stat, right_stat):
    square = (BLOCK, BLOCK)
    input_grad, left_next, right_next, update = whole_call(
        activations,
        cotangent,
        weight_blocks.reshape(square),
        left_stat.reshape(square),
        right_stat.reshape(square),
    )
    shape_out = left_stat.shape
    return (
        input_grad,
        left_next.reshape(shape_out),
        right_next.reshape(shape_out),
        update.reshape(shape_out),
    )


def solution(mesh):
    block = P("dp", "mp", "pre", None, None)
    return jax.shard_map(
        on_device,
        mesh=mesh,
        in_specs=(P("dp", "mp"), P("dp", "pre"), block, block, block),
        out_specs=(P("dp", ("mp", "pre")), block, block, block),
        check_vma=False,
    )
```

```python
import math

import jax
import jax.numpy as jnp
from jax import lax
from jax.experimental import pallas as pl
from jax.experimental.pallas import tpu as pltpu
from jax.sharding import PartitionSpec as P

D = 4096
FF = 16384
TOKENS = 4096
BLOCK = 512
NX, NY, NZ = 4, 4, 8

DECAY_RATE = 0.9
MESH = pl.DeviceIdType.MESH
DMA = pltpu.SemaphoreType.DMA
C0, C1, C2, C3 = 25 / 16, -(5 + 3125 / 256) / 16, 3125 / 4096, -1250 / 4096
C4, C5, C6 = 250 / 4096, -25 / 4096, 1 / 4096


def split(value):
    high = value.astype(jnp.bfloat16)
    return high, (value - high.astype(jnp.float32)).astype(jnp.bfloat16)


NN = (((1,), (0,)), ((), ()))
NT = (((1,), (1,)), ((), ()))
TN = (((0,), (0,)), ((), ()))


def dot(a, b, dims):
    return lax.dot_general(a, b, dims, preferred_element_type=jnp.float32)


def product(a, b, dims=NN):
    ah, al = a
    bh, bl = b
    return dot(ah, bh, dims) + (dot(ah, bl, dims) + dot(al, bh, dims))


def whole_kernel(
    act, cot, wblk, lstat, rstat,
    ig_out, left_out, right_out, update_out,
    ACT, OUTB, COT, CIG, WB, ACC, OB, G, GS, STAT, T2, T3, MS, CS, PS, RAW, RED,
    loc_sem, a1_s, a1_r, a1o_s, a1o_r, tz_s, tz_r, sw_s, sw_r,
    b1_s, b1_r, pa_s, pa_r, ring_s, ring_r, c1_s, c1_r, w_s, w_r, ws_s, ws_r, o_s, o_r,
    red_s, red_r, st_sem,
):
    dp = lax.axis_index("dp")
    y = lax.axis_index("mp")
    pre = lax.axis_index("pre")
    x = lax.div(dp, 4)
    zh = lax.rem(dp, 4)
    zl = lax.div(pre, 2)
    c = lax.rem(pre, 2)
    oc = 1 - c
    z = zh * 2 + zl
    grp = lax.div(z, 4)
    g = lax.rem(z, 4)
    side = lax.div(g, 2)
    inner = lax.rem(lax.div(g + 1, 2), 2)
    d = 1 - 2 * side
    so, sn, sf, se = 1 + side, 3 * side, 2 - side, 3 - 3 * side
    hpar = lax.rem(zh, 2)

    def dev(xx, yy, zz, cc):
        return {
            "dp": xx * 4 + lax.div(zz, 2),
            "mp": yy,
            "pre": lax.rem(zz, 2) * 2 + cc,
        }

    def xp(k):
        return lax.rem(x + k + 4, 4)

    def yp(k):
        return lax.rem(y + k + 4, 4)

    def zp(k):
        return lax.rem(z + k + 8, 8)

    def zp_d(sign):
        return lax.rem(z + sign * d + 8, 8)

    other = dev(x, y, z, oc)

    barrier = pltpu.get_barrier_semaphore()
    count = 0

    def greet(device):
        pl.semaphore_signal(barrier, inc=1, device_id=device, device_id_type=MESH)

    for k in range(4):
        for m in range(4):
            if k or m:
                greet({"dp": xp(k) * 4 + zh, "mp": y, "pre": lax.rem(pre + m, 4)})
                count += 1
    for k in range(1, 4):
        greet(dev(x, yp(k), z, c))
        count += 1
    pair = lax.rem(z + 1 - 2 * zl + 8, 8)
    for k in range(1, 7):
        greet(dev(x, y, lax.rem(pair + (1 - 2 * zl) * k + 16, 8), c))
        count += 1
    pl.semaphore_wait(barrier, count)

    sends = []
    branch = [None]

    def remote(src, dst, ssem, rsem, device, when=None):
        cp = pltpu.make_async_remote_copy(
            src_ref=src, dst_ref=dst, send_sem=ssem[0].at[ssem[1]], recv_sem=rsem,
            device_id=device, device_id_type=MESH,
        )
        if when is None:
            cp.start()
        else:
            pl.when(when)(cp.start)
        size = math.prod(dst.shape)
        sends.append((branch[0] if when is None else when, size, ssem))

    def arrived(dst, rsem):
        pltpu.make_async_copy(dst, dst, rsem).wait()

    is_inner = inner == 1
    is_outer = inner == 0

    def act_src(xx, gg):
        return act.at[
            pl.ds(pl.multiple_of(c * 128, 128), 128),
            pl.ds(pl.multiple_of(xx * 1024 + gg * 512, 512), 512),
        ]

    rel = (0, -1, 1, 2)
    xs = [xp(r) for r in rel]
    cot_piece = lambda half: cot.at[
        pl.ds(pl.multiple_of(y * 64, 64), 64),
        pl.ds(pl.multiple_of(half * 512, 512), 512),
    ]
    ypair = lax.div(y, 2)
    ylow = lax.rem(y, 2)
    cot_slot = lambda zz: COT.at[zz, ypair, x, ylow]
    pltpu.make_async_copy(cot_piece(hpar), cot_slot(zh), loc_sem.at[0]).start()
    remote(cot_piece(hpar), cot_slot(zh), (b1_s, (0,)), b1_r.at[0], dev(x, y, zp(4), c))
    remote(cot_piece(1 - hpar), cot_slot(zh), (b1_s, (1,)), b1_r.at[1], dev(x, y, zp(2), c))
    remote(cot_piece(1 - hpar), cot_slot(zh), (b1_s, (2,)), b1_r.at[2], dev(x, y, zp(-2), c))
    cig_src = lambda q: cot.at[pl.ds(pl.multiple_of(q * 64 + y * 16, 16), 16), :]

    def cig_sends():
        pltpu.make_async_copy(cig_src(pre), CIG.at[pre, x, y], loc_sem.at[3]).start()
        for k in range(1, 4):
            q = lax.rem(pre + k, 4)
            remote(cig_src(q), CIG.at[pre, x, y], (c1_s, (k,)), c1_r.at[k],
                   {"dp": dp, "mp": y, "pre": q})

    def act_sends():
        pltpu.make_async_copy(act_src(x, grp), ACT.at[so, c, x], loc_sem.at[1]).start()

        @pl.when(is_outer)
        def _():
            pltpu.make_async_copy(act_src(x, 1 - grp), OUTB.at[x], loc_sem.at[2]).start()

        steps = ((1, 1), (2, -1), (3, 2))
        for k, step in steps:
            to = xp(step)
            remote(act_src(to, 1 - grp), OUTB.at[x], (a1o_s, (k,)), a1o_r.at[k],
                   dev(to, y, z, c), when=is_outer)
        for k, step in steps:
            to = xp(step)
            remote(act_src(to, grp), ACT.at[so, c, x], (a1_s, (k,)), a1_r.at[k], dev(to, y, z, c))

    def ring_start(base, unit, my, to_next, to_prev):
        for hf in range(2):
            remote(unit(my, hf), unit(my, hf), (ring_s, (base + hf,)), ring_r.at[base + hf], to_next)
            back = 1 - hf
            remote(unit(my, back), unit(my, back), (ring_s, (base + 2 + back,)),
                   ring_r.at[base + 2 + back], to_prev)

    def ring_forward(base, unit, prv, nxt, to_next, to_prev):
        arrived(unit(prv, 0), ring_r.at[base])
        remote(unit(prv, 0), unit(prv, 0), (ring_s, (base + 4,)), ring_r.at[base + 4], to_next)
        arrived(unit(nxt, 1), ring_r.at[base + 3])
        remote(unit(nxt, 1), unit(nxt, 1), (ring_s, (base + 5,)), ring_r.at[base + 5], to_prev)

    def ring_end(base, unit, prv, nxt, far):
        arrived(unit(prv, 1), ring_r.at[base + 1])
        arrived(unit(nxt, 0), ring_r.at[base + 2])
        arrived(unit(far, 0), ring_r.at[base + 4])
        arrived(unit(far, 1), ring_r.at[base + 5])

    xnext, xprev = dev(xp(1), y, z, c), dev(xp(-1), y, z, c)
    ynext, yprev = dev(x, yp(1), z, c), dev(x, yp(-1), z, c)
    shards = [lax.rem(zh + r, 4) for r in range(4)]

    def cot_unit(r, i, lo):
        if r == 2:
            return COT.at[shards[r], lo, i]
        return COT.at[shards[r], lax.div(i, 2), pl.ds(2 * lo, 2), lax.rem(i, 2)]

    uc = lambda i, lo: CIG.at[pl.ds(2 * lo, 2), :, i]
    xargs = (xp(-1), xp(1), xnext, xprev)
    yargs = (yp(-1), yp(1), ynext, yprev)

    def cot_a(r):
        piece = cot_slot(shards[r])
        if r:
            arrived(piece, b1_r.at[{1: 2, 3: 1, 2: 0}[r]])
        for k in (2, 1, 3):
            to = dev(x, yp(k), z, c) if r == 2 else dev(xp(k), y, z, c)
            remote(piece if r else cot_piece(hpar), piece, (pa_s, (r, k,)), pa_r.at[r, k], to)

    def cot_b(r):
        for k in (1, 3, 2):
            if r == 2:
                arrived(COT.at[shards[r], lax.div(yp(-k), 2), x, lax.rem(yp(-k), 2)], pa_r.at[r, k])
            else:
                arrived(COT.at[shards[r], ypair, xp(-k), ylow], pa_r.at[r, k])
        if r == 0:
            pltpu.make_async_copy(cot_piece(hpar), cot_slot(zh), loc_sem.at[0]).wait()
        unit = lambda i, lo: cot_unit(r, i, lo)
        if r == 2:
            ring_start(6 * r, unit, x, xnext, xprev)
        else:
            ring_start(6 * r, unit, y, ynext, yprev)

    def cot_f(r):
        unit = lambda i, lo: cot_unit(r, i, lo)
        ring_forward(6 * r, unit, *(xargs if r == 2 else yargs))

    def cot_e(r):
        unit = lambda i, lo: cot_unit(r, i, lo)
        m = xp if r == 2 else yp
        ring_end(6 * r, unit, m(-1), m(1), m(2))

    def cig_a():
        pltpu.make_async_copy(cig_src(pre), CIG.at[pre, x, y], loc_sem.at[3]).wait()
        for k in range(1, 4):
            arrived(CIG.at[lax.rem(pre + 4 - k, 4), x, y], c1_r.at[k])
        for k in (2, 1, 3):
            piece = CIG.at[:, x, y]
            remote(piece, piece, (pa_s, (4, k)), pa_r.at[4, k], dev(xp(k), y, z, c))

    def cig_b():
        for k in (1, 3, 2):
            arrived(CIG.at[:, xp(-k), y], pa_r.at[4, k])
        ring_start(24, uc, y, ynext, yprev)

    def cig_f():
        ring_forward(24, uc, *yargs)

    def cig_e():
        ring_end(24, uc, yp(-1), yp(1), yp(2))

    inward = dev(x, y, zp_d(1), c)
    outward = dev(x, y, zp_d(-1), c)

    def swap(kind, k, slot):
        piece = ACT.at[slot, c, xs[k]]
        remote(piece, piece, (sw_s, (kind, k,)), sw_r.at[kind, k], other)

    def own(k):
        piece = ACT.at[so, c, xs[k]]
        if branch[0] is is_outer:
            if k == 0:
                pltpu.make_async_copy(act_src(x, 1 - grp), OUTB.at[x], loc_sem.at[2]).wait()
            else:
                arrived(OUTB.at[xs[k]], a1o_r.at[k])
            remote(OUTB.at[xs[k]], ACT.at[3 - sn, c, xs[k]],
                   (tz_s, (0, k,)), tz_r.at[0, k], outward)
        else:
            own_here(k, piece)
            remote(piece, piece, (tz_s, (1, k,)), tz_r.at[1, k], inward)

    def own_here(k, piece):
        if k == 0:
            pltpu.make_async_copy(act_src(x, grp), piece, loc_sem.at[1]).wait()
        else:
            arrived(piece, a1_r.at[k])

    def own_swap(k):
        piece = ACT.at[so, c, xs[k]]
        if branch[0] is is_outer:
            own_here(k, piece)
        swap(3, k, so)

    def near(k):
        piece = ACT.at[sn, c, xs[k]]
        arrived(piece, tz_r.at[0, k])
        remote(piece, piece, (tz_s, (2, k,)),
               tz_r.at[0 if branch[0] is is_outer else 2, k], inward)
        swap(0, k, sn)

    def far(k):
        piece = ACT.at[sf, c, xs[k]]
        arrived(piece, tz_r.at[1, k])
        if branch[0] is is_inner:
            remote(piece, piece, (tz_s, (3, k,)), tz_r.at[1, k], outward)
        swap(1, k, sf)

    def end(k):
        piece = ACT.at[se, c, xs[k]]
        arrived(piece, tz_r.at[2, k])
        if branch[0] is is_inner:
            remote(piece, piece, (tz_s, (4, k,)), tz_r.at[2, k], outward)
        swap(2, k, se)

    znext, zprev = dev(x, y, zp(1), c), dev(x, y, zp(-1), c)
    wpart = lambda zz, hf: WB.at[zz, c, pl.ds(hf * 256, 256)]

    def w_send(way, t, hf):
        zz = zp(-(t - 1)) if way == 0 else zp(t - 1)
        remote(wblk.at[pl.ds(hf * 256, 256)] if t == 1 else wpart(zz, hf), wpart(zz, hf),
               (w_s, (way, t, hf,)), w_r.at[way, t, hf], znext if way == 0 else zprev)

    def w_index(way, t, hf):
        return 1 + (way * 5 + t) * 2 + hf

    def w_arrive(way, t, hf):
        zz = zp(-t) if way == 0 else zp(t)
        arrived(wpart(zz, hf), w_r.at[way, t, hf])
        if t < 3 or (t == 3 and hf == way):
            w_send(way, t + 1, hf)
        n = w_index(way, t, hf)
        remote(wpart(zz, hf), wpart(zz, hf), (ws_s, (n,)), ws_r.at[n], other)

    def w_first():
        pltpu.make_async_copy(wblk, WB.at[z, c], loc_sem.at[4]).start()
        remote(wblk, WB.at[z, c], (ws_s, (0,)), ws_r.at[0], other)
        for hf in range(2):
            for way in range(2):
                w_send(way, 1, hf)

    def w_half(t, hf):
        for way in range(2):
            if t < 4 or hf == way:
                w_arrive(way, t, hf)

    def ig_chip(zz):
        for cc in range(2):
            p = lax.rem(zz, 2) * 2 + cc
            h = lax.rem(lax.div(zz, 2), 2)
            a = CIG[p, :, :, :, pl.ds(pl.multiple_of(h * 512, 512), 512)].reshape(256, 512)
            ACC[lax.div(zz, 4)] += dot(a, WB[zz, cc], NT)

    def ig_own():
        pltpu.make_async_copy(wblk, WB.at[z, c], loc_sem.at[4]).wait()
        arrived(WB.at[z, oc], ws_r.at[0])
        ACC[...] = jnp.zeros_like(ACC)
        ig_chip(z)

    def ig_wait(way, t):
        zz = zp(-t) if way == 0 else zp(t)
        for hf in range(2):
            if t < 4 or hf == way:
                arrived(WB.at[zz, oc, pl.ds(hf * 256, 256)], ws_r.at[w_index(way, t, hf)])

    def ig_step(t):
        for way in range(2):
            ig_wait(way, t)
            if t < 4:
                ig_chip(zp(-t) if way == 0 else zp(t))
        if t == 4:
            ig_chip(zp(4))

    def gradient():
        for kind, slot in ((3, so), (0, sn), (1, sf), (2, se)):
            for k in range(4):
                arrived(ACT.at[slot, oc, xs[k]], sw_r.at[kind, k])
        G[...] = jnp.zeros_like(G)

        @pl.loop(0, 8)
        def _(i):
            s = lax.div(i, 2)
            cc = lax.rem(i, 2)
            shard = lax.rem(2 * grp + 3 + s, 4)
            a = ACT[s, cc].reshape(BLOCK, BLOCK)
            b = COT[shard, cc].reshape(BLOCK, BLOCK)
            G[...] += dot(a, b, TN)

        grad = G[...] * (1.0 / TOKENS)
        high, low = split(grad)
        GS[0] = high
        GS[1] = low

    pair_of = lambda ref: (ref[0], ref[1])

    def put(ref, value):
        high, low = split(value)
        ref[0] = high
        ref[1] = low

    def statistic(i, dims, old, new):
        pltpu.make_async_copy(old, STAT.at[i], st_sem.at[i]).wait()
        g = pair_of(GS)
        STAT[i] = DECAY_RATE * STAT[i] + (1.0 - DECAY_RATE) * product(g, g, dims)
        cp = pltpu.make_async_copy(STAT.at[i], new, st_sem.at[2 + i])
        cp.start()
        local_out.append(cp)

    scale = [None, None]

    def root_1(i):
        a = STAT[i]
        z_of = 2.5 * lax.rsqrt(jnp.sum(a * a, axis=(0, 1), keepdims=True))
        scale[i] = z_of
        put(MS, z_of * a)
        T2[...] = product(pair_of(MS), pair_of(MS))
        put(CS, T2[...])

    def root_2(i):
        T3[...] = product(pair_of(MS), pair_of(CS))

    def root_3(i):
        m = scale[i] * STAT[i]
        put(CS, C4 * m + C5 * T2[...] + C6 * T3[...])
        put(MS, T3[...])
        eye = (
            lax.broadcasted_iota(jnp.int32, (BLOCK, BLOCK), 0)
            == lax.broadcasted_iota(jnp.int32, (BLOCK, BLOCK), 1)
        )
        low_part = C1 * m + C2 * T2[...] + C3 * T3[...] + jnp.where(eye, C0, 0.0)
        whole = low_part + product(pair_of(MS), pair_of(CS))
        put(PS.at[i], jnp.sqrt(jnp.sqrt(scale[i])) * whole)

    def raw_1():
        put(CS, product(pair_of(PS.at[0]), pair_of(GS)))

    def raw_2():
        raw = product(pair_of(CS), pair_of(PS.at[1]))
        RAW[...] = raw
        RED[0] = jnp.broadcast_to(jnp.sum(raw * raw, axis=(0, 1), keepdims=True), (8, 128))

    def red_targets(stage):
        if stage == 0:
            return [(1, other)]
        if stage == 1:
            return [(1 + k, dev(x, y, zp(k), c)) for k in range(1, 8)]
        if stage == 2:
            return [(8 + k, dev(xp(k), y, z, c)) for k in range(1, 4)]
        return [(11 + k, dev(x, yp(k), z, c)) for k in range(1, 4)]

    def red_send(stage):
        for slot, device in red_targets(stage):
            remote(RED.at[15 + stage], RED.at[slot], (red_s, (slot,)), red_r.at[slot], device)

    def red_start(stage):
        RED[15 + stage] = RED[0]
        red_send(stage)

    def red_finish(stage):
        total = RED[0]
        for slot, _ in red_targets(stage):
            arrived(RED.at[slot], red_r.at[slot])
            total = total + RED[slot]
        RED[0] = total

    def update():
        mean_square = RED[0, 0:1, 0:1] * (1.0 / (FF * D))
        RAW[...] = RAW[...] * lax.rsqrt(mean_square + 1e-06)
        cp = pltpu.make_async_copy(RAW, update_out, st_sem.at[4])
        cp.start()
        local_out.append(cp)

    local_out = []
    pltpu.make_async_copy(lstat, STAT.at[0], st_sem.at[0]).start()
    pltpu.make_async_copy(rstat, STAT.at[1], st_sem.at[1]).start()

    cot_a(0)
    act_sends()
    cig_sends()

    @pl.when(is_inner)
    def _():
        branch[0] = is_inner
        own(0)
        cot_b(0)
        own(1)
        own(2)
        far(0)
        cot_a(1)
        cot_a(3)
        own(3)
        far(1)
        near(0)
        far(2)
        cot_a(2)
        cot_b(1)
        near(1)
        far(3)
        cot_f(0)
        cot_b(3)
        near(2)
        end(0)
        cot_b(2)
        near(3)
        end(1)
        cot_f(1)
        end(2)
        end(3)
        cot_f(3)
        cot_f(2)
        cig_a()
        own_swap(0)
        own_swap(1)
        own_swap(2)
        own_swap(3)

    @pl.when(is_outer)
    def _():
        branch[0] = is_outer
        own(0)
        cot_b(0)
        own(1)
        own(2)
        cot_a(1)
        cot_a(3)
        own(3)
        near(0)
        near(1)
        far(0)
        cot_a(2)
        cot_b(1)
        near(2)
        far(1)
        cot_f(0)
        near(3)
        cot_b(3)
        far(2)
        end(0)
        cot_b(2)
        far(3)
        end(1)
        cot_f(1)
        end(2)
        end(3)
        cot_f(3)
        cot_f(2)
        cig_a()
        own_swap(0)
        own_swap(1)
        own_swap(2)
        own_swap(3)

    branch[0] = None
    w_first()
    cot_e(0)
    cot_e(1)
    cot_e(3)
    cot_e(2)
    cig_b()
    gradient()
    statistic(0, NT, lstat, left_out)
    statistic(1, TN, rstat, right_out)
    w_half(1, 0)
    root_1(0)
    root_2(0)
    root_3(0)
    w_half(1, 1)
    cig_f()
    root_1(1)
    root_2(1)
    root_3(1)
    raw_1()
    w_half(2, 0)
    raw_2()
    red_start(0)
    red_finish(0)
    red_start(1)
    cig_e()
    ig_own()
    w_half(2, 1)
    red_finish(1)
    red_start(2)
    ig_step(1)
    w_half(3, 0)
    red_finish(2)
    red_start(3)
    ig_step(2)
    w_half(3, 1)
    red_finish(3)
    update()
    ig_step(3)
    w_half(4, 0)
    w_half(4, 1)
    ig_step(4)

    for j in range(2):
        OB[:, :, pl.ds(j * 512, 512)] = ACC[j].reshape(4, 64, 512).astype(jnp.bfloat16)
    sub = zl * 2 + c
    z_to = zh * 2 + lax.div(x, 2)
    c_to = lax.rem(x, 2)
    rows = ig_out.at[pl.ds(pl.multiple_of(sub * 64, 64), 64), :]
    mine = pre == x
    not_mine = jnp.logical_not(mine)
    for k in range(4):
        xt = xs[k]
        dst = dev(xt, y, z_to, c_to)
        if k == 0:
            remote(OB.at[xt], rows, (o_s, (k,)), o_r.at[sub], dst, when=not_mine)

            @pl.when(mine)
            def _():
                cp = pltpu.make_async_copy(OB.at[x], rows, loc_sem.at[5])
                cp.start()
                cp.wait()
        else:
            remote(OB.at[xt], rows, (o_s, (k,)), o_r.at[sub], dst)
    for q in range(4):
        piece = ig_out.at[pl.ds(q * 64, 64), :]

        @pl.when(jnp.logical_not(jnp.logical_and(mine, sub == q)))
        def _():
            arrived(piece, o_r.at[q])

    for cp in local_out:
        cp.wait()
    def sent(size, ssem):
        same = RED.at[0] if size == 1024 else WB.at[0, 0, pl.ds(0, size // 512)]
        pltpu.make_async_remote_copy(
            src_ref=same, dst_ref=same, send_sem=ssem[0].at[ssem[1]], recv_sem=o_r.at[0],
            device_id=other, device_id_type=MESH,
        ).wait_send()

    for flag in (None, is_inner, is_outer, not_mine):
        group = [entry[1:] for entry in sends if entry[0] is flag]

        def drain(group=group):
            for entry in group:
                sent(*entry)

        if flag is None:
            drain()
        else:
            pl.when(flag)(drain)


def whole_call(act, cot, wblk, lstat, rstat):
    any_spec = pl.BlockSpec(memory_space=pl.ANY)
    bf, f32 = jnp.bfloat16, jnp.float32
    square = jax.ShapeDtypeStruct((BLOCK, BLOCK), f32)
    return pl.pallas_call(
        whole_kernel,
        out_shape=(jax.ShapeDtypeStruct((256, 1024), bf), square, square, square),
        in_specs=[any_spec] * 5,
        out_specs=(any_spec,) * 4,
        scratch_shapes=[
            pltpu.VMEM((4, 2, 4, 128, 512), bf),
            pltpu.VMEM((4, 128, 512), bf),
            pltpu.VMEM((4, 2, 4, 2, 64, 512), bf),
            pltpu.VMEM((4, 4, 4, 16, 1024), bf),
            pltpu.VMEM((8, 2, 512, 512), bf),
            pltpu.VMEM((2, 256, 512), f32),
            pltpu.VMEM((4, 64, 1024), bf),
            pltpu.VMEM((BLOCK, BLOCK), f32),
            pltpu.VMEM((2, BLOCK, BLOCK), bf),
            pltpu.VMEM((2, BLOCK, BLOCK), f32),
            pltpu.VMEM((BLOCK, BLOCK), f32),
            pltpu.VMEM((BLOCK, BLOCK), f32),
            pltpu.VMEM((2, BLOCK, BLOCK), bf),
            pltpu.VMEM((2, BLOCK, BLOCK), bf),
            pltpu.VMEM((2, 2, BLOCK, BLOCK), bf),
            pltpu.VMEM((BLOCK, BLOCK), f32),
            pltpu.VMEM((19, 8, 128), f32),
            DMA((6,)), DMA((4,)), DMA((4,)), DMA((4,)), DMA((4,)),
            DMA((5, 4)), DMA((3, 4)), DMA((4, 4)), DMA((4, 4)),
            DMA((3,)), DMA((3,)), DMA((5, 4)), DMA((5, 4)), DMA((30,)), DMA((30,)),
            DMA((4,)), DMA((4,)), DMA((2, 5, 2)), DMA((2, 5, 2)), DMA((21,)), DMA((21,)),
            DMA((4,)), DMA((4,)), DMA((15,)), DMA((15,)), DMA((5,)),
        ],
        compiler_params=pltpu.CompilerParams(
            collective_id=0, has_side_effects=True, vmem_limit_bytes=60 * 1024 * 1024
        ),
        name="gather_products",
    )(act, cot, wblk, lstat, rstat)


def copy_kernel(*refs):
    n = (len(refs) - 2) // 3
    src, dst, held = refs[:n], refs[n : 2 * n], refs[2 * n : 3 * n]
    into = [pltpu.make_async_copy(src[i], held[i], refs[-2].at[i]) for i in range(n)]
    out = [pltpu.make_async_copy(held[i], dst[i], refs[-1].at[i]) for i in range(n)]
    for cp in into:
        cp.start()
    for i in range(n):
        into[i].wait()
        out[i].start()
    for cp in out:
        cp.wait()


def place(*arrays):
    any_spec = pl.BlockSpec(memory_space=pl.ANY)
    n = len(arrays)
    return pl.pallas_call(
        copy_kernel,
        out_shape=tuple(jax.ShapeDtypeStruct(a.shape, a.dtype) for a in arrays),
        in_specs=[any_spec] * n,
        out_specs=(any_spec,) * n,
        scratch_shapes=[pltpu.VMEM(a.shape, a.dtype) for a in arrays] + [DMA((n,)), DMA((n,))],
        compiler_params=pltpu.CompilerParams(vmem_limit_bytes=60 * 1024 * 1024),
        name="place",
    )(*arrays)


def on_device(activations, cotangent, weight_blocks, left_stat, right_stat):
    square = (BLOCK, BLOCK)
    input_grad, left_next, right_next, update = whole_call(
        activations,
        cotangent,
        weight_blocks.reshape(square),
        left_stat.reshape(square),
        right_stat.reshape(square),
    )
    input_grad, left_next, right_next, update = place(
        input_grad, left_next, right_next, update
    )
    shape_out = left_stat.shape
    return (
        input_grad,
        left_next.reshape(shape_out),
        right_next.reshape(shape_out),
        update.reshape(shape_out),
    )


def solution(mesh):
    block = P("dp", "mp", "pre", None, None)
    return jax.shard_map(
        on_device,
        mesh=mesh,
        in_specs=(P("dp", "mp"), P("dp", "pre"), block, block, block),
        out_specs=(P("dp", ("mp", "pre")), block, block, block),
        check_vma=False,
    )
```

```python
import math

import jax
import jax.numpy as jnp
from jax import lax
from jax.experimental import pallas as pl
from jax.experimental.pallas import tpu as pltpu
from jax.sharding import PartitionSpec as P

D = 4096
FF = 16384
TOKENS = 4096
BLOCK = 512
NX, NY, NZ = 4, 4, 8

DECAY_RATE = 0.9
MESH = pl.DeviceIdType.MESH
DMA = pltpu.SemaphoreType.DMA
C0, C1, C2, C3 = 25 / 16, -(5 + 3125 / 256) / 16, 3125 / 4096, -1250 / 4096
C4, C5, C6 = 250 / 4096, -25 / 4096, 1 / 4096


def split(value):
    high = value.astype(jnp.bfloat16)
    return high, (value - high.astype(jnp.float32)).astype(jnp.bfloat16)


NN = (((1,), (0,)), ((), ()))
NT = (((1,), (1,)), ((), ()))
TN = (((0,), (0,)), ((), ()))


def dot(a, b, dims):
    return lax.dot_general(a, b, dims, preferred_element_type=jnp.float32)


def product(a, b, dims=NN):
    ah, al = a
    bh, bl = b
    return dot(ah, bh, dims) + (dot(ah, bl, dims) + dot(al, bh, dims))


def whole_kernel(
    act, cot, wblk, lstat, rstat,
    ig_out, left_out, right_out, update_out,
    ACT, OUTB, COT, CIG, WB, ACC, OB, G, GS, STAT, T2, T3, MS, CS, PS, RAW, RED, HOP,
    loc_sem, a1_s, a1_r, a1o_s, a1o_r, tz_s, tz_r, sw_s, sw_r,
    b1_s, b1_r, pa_s, pa_r, ring_s, ring_r, c1_s, c1_r, w_s, w_r, ws_s, ws_r, o_s, o_r,
    red_s, red_r, st_sem, hop_s, hop_r,
):
    dp = lax.axis_index("dp")
    y = lax.axis_index("mp")
    pre = lax.axis_index("pre")
    x = lax.div(dp, 4)
    zh = lax.rem(dp, 4)
    zl = lax.div(pre, 2)
    c = lax.rem(pre, 2)
    oc = 1 - c
    z = zh * 2 + zl
    grp = lax.div(z, 4)
    g = lax.rem(z, 4)
    side = lax.div(g, 2)
    inner = lax.rem(lax.div(g + 1, 2), 2)
    d = 1 - 2 * side
    so, sn, sf, se = 1 + side, 3 * side, 2 - side, 3 - 3 * side
    hpar = lax.rem(zh, 2)

    def dev(xx, yy, zz, cc):
        return {
            "dp": xx * 4 + lax.div(zz, 2),
            "mp": yy,
            "pre": lax.rem(zz, 2) * 2 + cc,
        }

    def xp(k):
        return lax.rem(x + k + 4, 4)

    def yp(k):
        return lax.rem(y + k + 4, 4)

    def zp(k):
        return lax.rem(z + k + 8, 8)

    def zp_d(sign):
        return lax.rem(z + sign * d + 8, 8)

    other = dev(x, y, z, oc)

    barrier = pltpu.get_barrier_semaphore()
    count = 0

    def greet(device):
        pl.semaphore_signal(barrier, inc=1, device_id=device, device_id_type=MESH)

    for k in range(1, 4):
        greet({"dp": dp, "mp": y, "pre": lax.rem(pre + k, 4)})
        greet(dev(xp(k), y, z, c))
        greet(dev(xp(k), y, z, oc))
        count += 3
    for k in range(1, 4):
        greet(dev(x, yp(k), z, c))
        count += 1
    pair = lax.rem(z + 1 - 2 * zl + 8, 8)
    for k in range(1, 7):
        greet(dev(x, y, lax.rem(pair + (1 - 2 * zl) * k + 16, 8), c))
        count += 1
    pl.semaphore_wait(barrier, count)

    sends = []
    branch = [None]

    def remote(src, dst, ssem, rsem, device, when=None):
        cp = pltpu.make_async_remote_copy(
            src_ref=src, dst_ref=dst, send_sem=ssem[0].at[ssem[1]], recv_sem=rsem,
            device_id=device, device_id_type=MESH,
        )
        if when is None:
            cp.start()
        else:
            pl.when(when)(cp.start)
        size = math.prod(dst.shape)
        sends.append((branch[0] if when is None else when, size, ssem))

    def arrived(dst, rsem):
        pltpu.make_async_copy(dst, dst, rsem).wait()

    is_inner = inner == 1
    is_outer = inner == 0

    def act_src(xx, gg):
        return act.at[
            pl.ds(pl.multiple_of(c * 128, 128), 128),
            pl.ds(pl.multiple_of(xx * 1024 + gg * 512, 512), 512),
        ]

    rel = (0, -1, 1, 2)
    xs = [xp(r) for r in rel]
    cot_piece = lambda half: cot.at[
        pl.ds(pl.multiple_of(y * 64, 64), 64),
        pl.ds(pl.multiple_of(half * 512, 512), 512),
    ]
    ypair = lax.div(y, 2)
    ylow = lax.rem(y, 2)
    cot_slot = lambda zz: COT.at[zz, ypair, x, ylow]
    pltpu.make_async_copy(cot_piece(hpar), cot_slot(zh), loc_sem.at[0]).start()
    remote(cot_piece(hpar), cot_slot(zh), (b1_s, (0,)), b1_r.at[0], dev(x, y, zp(4), c))
    remote(cot_piece(1 - hpar), cot_slot(zh), (b1_s, (1,)), b1_r.at[1], dev(x, y, zp(2), c))
    remote(cot_piece(1 - hpar), cot_slot(zh), (b1_s, (2,)), b1_r.at[2], dev(x, y, zp(-2), c))
    cig_src = lambda q: cot.at[pl.ds(pl.multiple_of(q * 64 + y * 16, 16), 16), :]

    def cig_sends():
        pltpu.make_async_copy(cig_src(pre), CIG.at[pre, x, y], loc_sem.at[3]).start()
        for k in range(1, 4):
            q = lax.rem(pre + k, 4)
            remote(cig_src(q), CIG.at[pre, x, y], (c1_s, (k,)), c1_r.at[k],
                   {"dp": dp, "mp": y, "pre": q})

    def act_sends():
        pltpu.make_async_copy(act_src(x, grp), ACT.at[so, c, x], loc_sem.at[1]).start()

        @pl.when(is_outer)
        def _():
            pltpu.make_async_copy(act_src(x, 1 - grp), OUTB.at[x], loc_sem.at[2]).start()

        steps = ((1, 1), (2, -1), (3, 2))
        for k, step in steps:
            to = xp(step)
            remote(act_src(to, 1 - grp), OUTB.at[x], (a1o_s, (k,)), a1o_r.at[k],
                   dev(to, y, z, c), when=is_outer)
        for k, step in steps:
            to = xp(step)
            remote(act_src(to, grp), ACT.at[so, c, x], (a1_s, (k,)), a1_r.at[k], dev(to, y, z, c))

    def ring_start(base, unit, my, to_next, to_prev):
        for hf in range(2):
            remote(unit(my, hf), unit(my, hf), (ring_s, (base + hf,)), ring_r.at[base + hf], to_next)
            back = 1 - hf
            remote(unit(my, back), unit(my, back), (ring_s, (base + 2 + back,)),
                   ring_r.at[base + 2 + back], to_prev)

    def ring_forward(base, unit, prv, nxt, to_next, to_prev):
        arrived(unit(prv, 0), ring_r.at[base])
        remote(unit(prv, 0), unit(prv, 0), (ring_s, (base + 4,)), ring_r.at[base + 4], to_next)
        arrived(unit(nxt, 1), ring_r.at[base + 3])
        remote(unit(nxt, 1), unit(nxt, 1), (ring_s, (base + 5,)), ring_r.at[base + 5], to_prev)

    def ring_end(base, unit, prv, nxt, far):
        arrived(unit(prv, 1), ring_r.at[base + 1])
        arrived(unit(nxt, 0), ring_r.at[base + 2])
        arrived(unit(far, 0), ring_r.at[base + 4])
        arrived(unit(far, 1), ring_r.at[base + 5])

    xnext, xprev = dev(xp(1), y, z, c), dev(xp(-1), y, z, c)
    ynext, yprev = dev(x, yp(1), z, c), dev(x, yp(-1), z, c)
    shards = [lax.rem(zh + r, 4) for r in range(4)]

    def cot_unit(r, i, lo):
        if r == 2:
            return COT.at[shards[r], lo, i]
        return COT.at[shards[r], lax.div(i, 2), pl.ds(2 * lo, 2), lax.rem(i, 2)]

    uc = lambda i, lo: CIG.at[pl.ds(2 * lo, 2), :, i]
    xargs = (xp(-1), xp(1), xnext, xprev)
    yargs = (yp(-1), yp(1), ynext, yprev)

    def cot_a(r):
        piece = cot_slot(shards[r])
        if r:
            arrived(piece, b1_r.at[{1: 2, 3: 1, 2: 0}[r]])
        for k in (2, 1, 3):
            to = dev(x, yp(k), z, c) if r == 2 else dev(xp(k), y, z, c)
            remote(piece if r else cot_piece(hpar), piece, (pa_s, (r, k,)), pa_r.at[r, k], to)

    def cot_b(r):
        for k in (1, 3, 2):
            if r == 2:
                arrived(COT.at[shards[r], lax.div(yp(-k), 2), x, lax.rem(yp(-k), 2)], pa_r.at[r, k])
            else:
                arrived(COT.at[shards[r], ypair, xp(-k), ylow], pa_r.at[r, k])
        if r == 0:
            pltpu.make_async_copy(cot_piece(hpar), cot_slot(zh), loc_sem.at[0]).wait()
        unit = lambda i, lo: cot_unit(r, i, lo)
        if r == 2:
            ring_start(6 * r, unit, x, xnext, xprev)
        else:
            ring_start(6 * r, unit, y, ynext, yprev)

    def cot_f(r):
        unit = lambda i, lo: cot_unit(r, i, lo)
        ring_forward(6 * r, unit, *(xargs if r == 2 else yargs))

    def cot_e(r):
        unit = lambda i, lo: cot_unit(r, i, lo)
        m = xp if r == 2 else yp
        ring_end(6 * r, unit, m(-1), m(1), m(2))

    def cig_a():
        pltpu.make_async_copy(cig_src(pre), CIG.at[pre, x, y], loc_sem.at[3]).wait()
        for k in range(1, 4):
            arrived(CIG.at[lax.rem(pre + 4 - k, 4), x, y], c1_r.at[k])
        for k in (2, 1, 3):
            piece = CIG.at[:, x, y]
            remote(piece, piece, (pa_s, (4, k)), pa_r.at[4, k], dev(xp(k), y, z, c))

    def cig_b():
        for k in (1, 3, 2):
            arrived(CIG.at[:, xp(-k), y], pa_r.at[4, k])
        ring_start(24, uc, y, ynext, yprev)

    def cig_f():
        ring_forward(24, uc, *yargs)

    def cig_e():
        ring_end(24, uc, yp(-1), yp(1), yp(2))

    inward = dev(x, y, zp_d(1), c)
    outward = dev(x, y, zp_d(-1), c)

    def swap(kind, k, slot):
        piece = ACT.at[slot, c, xs[k]]
        remote(piece, piece, (sw_s, (kind, k,)), sw_r.at[kind, k], other)

    def own(k):
        piece = ACT.at[so, c, xs[k]]
        if branch[0] is is_outer:
            if k == 0:
                pltpu.make_async_copy(act_src(x, 1 - grp), OUTB.at[x], loc_sem.at[2]).wait()
            else:
                arrived(OUTB.at[xs[k]], a1o_r.at[k])
            remote(OUTB.at[xs[k]], ACT.at[3 - sn, c, xs[k]],
                   (tz_s, (0, k,)), tz_r.at[0, k], outward)
        else:
            own_here(k, piece)
            remote(piece, piece, (tz_s, (1, k,)), tz_r.at[1, k], inward)

    def own_here(k, piece):
        if k == 0:
            pltpu.make_async_copy(act_src(x, grp), piece, loc_sem.at[1]).wait()
        else:
            arrived(piece, a1_r.at[k])

    def own_swap(k):
        piece = ACT.at[so, c, xs[k]]
        if branch[0] is is_outer:
            own_here(k, piece)
        swap(3, k, so)

    def near(k):
        piece = ACT.at[sn, c, xs[k]]
        arrived(piece, tz_r.at[0, k])
        remote(piece, piece, (tz_s, (2, k,)),
               tz_r.at[0 if branch[0] is is_outer else 2, k], inward)
        swap(0, k, sn)

    def far(k):
        piece = ACT.at[sf, c, xs[k]]
        arrived(piece, tz_r.at[1, k])
        if branch[0] is is_inner:
            remote(piece, piece, (tz_s, (3, k,)), tz_r.at[1, k], outward)
        swap(1, k, sf)

    def end(k):
        piece = ACT.at[se, c, xs[k]]
        arrived(piece, tz_r.at[2, k])
        if branch[0] is is_inner:
            remote(piece, piece, (tz_s, (4, k,)), tz_r.at[2, k], outward)
        swap(2, k, se)

    znext, zprev = dev(x, y, zp(1), c), dev(x, y, zp(-1), c)
    wpart = lambda zz, hf: WB.at[zz, c, pl.ds(hf * 256, 256)]

    def w_send(way, t, hf):
        zz = zp(-(t - 1)) if way == 0 else zp(t - 1)
        remote(wblk.at[pl.ds(hf * 256, 256)] if t == 1 else wpart(zz, hf), wpart(zz, hf),
               (w_s, (way, t, hf,)), w_r.at[way, t, hf], znext if way == 0 else zprev)

    def w_index(way, t, hf):
        return 1 + (way * 5 + t) * 2 + hf

    def w_arrive(way, t, hf):
        zz = zp(-t) if way == 0 else zp(t)
        arrived(wpart(zz, hf), w_r.at[way, t, hf])
        if t < 3 or (t == 3 and hf == way):
            w_send(way, t + 1, hf)
        n = w_index(way, t, hf)
        remote(wpart(zz, hf), wpart(zz, hf), (ws_s, (n,)), ws_r.at[n], other)

    def w_first():
        pltpu.make_async_copy(wblk, WB.at[z, c], loc_sem.at[4]).start()
        remote(wblk, WB.at[z, c], (ws_s, (0,)), ws_r.at[0], other)
        for hf in range(2):
            for way in range(2):
                w_send(way, 1, hf)

    def w_half(t, hf):
        for way in range(2):
            if t < 4 or hf == way:
                w_arrive(way, t, hf)

    def ig_chip(zz):
        for cc in range(2):
            p = lax.rem(zz, 2) * 2 + cc
            h = lax.rem(lax.div(zz, 2), 2)
            a = CIG[p, :, :, :, pl.ds(pl.multiple_of(h * 512, 512), 512)].reshape(256, 512)
            ACC[lax.div(zz, 4)] += dot(a, WB[zz, cc], NT)

    def ig_own():
        pltpu.make_async_copy(wblk, WB.at[z, c], loc_sem.at[4]).wait()
        arrived(WB.at[z, oc], ws_r.at[0])
        ACC[...] = jnp.zeros_like(ACC)
        ig_chip(z)

    def ig_wait(way, t):
        zz = zp(-t) if way == 0 else zp(t)
        for hf in range(2):
            if t < 4 or hf == way:
                arrived(WB.at[zz, oc, pl.ds(hf * 256, 256)], ws_r.at[w_index(way, t, hf)])

    def ig_step(t):
        for way in range(2):
            ig_wait(way, t)
            if t < 4:
                ig_chip(zp(-t) if way == 0 else zp(t))
        if t == 4:
            ig_chip(zp(4))

    def gradient():
        for kind, slot in ((3, so), (0, sn), (1, sf), (2, se)):
            for k in range(4):
                arrived(ACT.at[slot, oc, xs[k]], sw_r.at[kind, k])
        G[...] = jnp.zeros_like(G)

        @pl.loop(0, 8)
        def _(i):
            s = lax.div(i, 2)
            cc = lax.rem(i, 2)
            shard = lax.rem(2 * grp + 3 + s, 4)
            a = ACT[s, cc].reshape(BLOCK, BLOCK)
            b = COT[shard, cc].reshape(BLOCK, BLOCK)
            G[...] += dot(a, b, TN)

        grad = G[...] * (1.0 / TOKENS)
        high, low = split(grad)
        GS[0] = high
        GS[1] = low

    pair_of = lambda ref: (ref[0], ref[1])

    def put(ref, value):
        high, low = split(value)
        ref[0] = high
        ref[1] = low

    def statistic(i, dims, old, new):
        pltpu.make_async_copy(old, STAT.at[i], st_sem.at[i]).wait()
        g = pair_of(GS)
        STAT[i] = DECAY_RATE * STAT[i] + (1.0 - DECAY_RATE) * product(g, g, dims)
        cp = pltpu.make_async_copy(STAT.at[i], new, st_sem.at[2 + i])
        cp.start()
        local_out.append(cp)

    scale = [None, None]

    def root_1(i):
        a = STAT[i]
        z_of = 2.5 * lax.rsqrt(jnp.sum(a * a, axis=(0, 1), keepdims=True))
        scale[i] = z_of
        put(MS, z_of * a)
        T2[...] = product(pair_of(MS), pair_of(MS))
        put(CS, T2[...])

    def root_2(i):
        T3[...] = product(pair_of(MS), pair_of(CS))

    def root_3(i):
        m = scale[i] * STAT[i]
        put(CS, C4 * m + C5 * T2[...] + C6 * T3[...])
        put(MS, T3[...])
        eye = (
            lax.broadcasted_iota(jnp.int32, (BLOCK, BLOCK), 0)
            == lax.broadcasted_iota(jnp.int32, (BLOCK, BLOCK), 1)
        )
        low_part = C1 * m + C2 * T2[...] + C3 * T3[...] + jnp.where(eye, C0, 0.0)
        whole = low_part + product(pair_of(MS), pair_of(CS))
        put(PS.at[i], jnp.sqrt(jnp.sqrt(scale[i])) * whole)

    def raw_1():
        put(CS, product(pair_of(PS.at[0]), pair_of(GS)))

    def raw_2():
        raw = product(pair_of(CS), pair_of(PS.at[1]))
        RAW[...] = raw
        RED[0] = jnp.broadcast_to(jnp.sum(raw * raw, axis=(0, 1), keepdims=True), (8, 128))

    def red_targets(stage):
        if stage == 0:
            return [(1, other)]
        if stage == 1:
            return [(1 + k, dev(x, y, zp(k), c)) for k in range(1, 8)]
        if stage == 2:
            return [(8 + k, dev(xp(k), y, z, c)) for k in range(1, 4)]
        return [(11 + k, dev(x, yp(k), z, c)) for k in range(1, 4)]

    def red_send(stage):
        for slot, device in red_targets(stage):
            remote(RED.at[15 + stage], RED.at[slot], (red_s, (slot,)), red_r.at[slot], device)

    def red_start(stage):
        RED[15 + stage] = RED[0]
        red_send(stage)

    def red_finish(stage):
        total = RED[0]
        for slot, _ in red_targets(stage):
            arrived(RED.at[slot], red_r.at[slot])
            total = total + RED[slot]
        RED[0] = total

    def update():
        mean_square = RED[0, 0:1, 0:1] * (1.0 / (FF * D))
        RAW[...] = RAW[...] * lax.rsqrt(mean_square + 1e-06)
        cp = pltpu.make_async_copy(RAW, update_out, st_sem.at[4])
        cp.start()
        local_out.append(cp)

    local_out = []
    pltpu.make_async_copy(lstat, STAT.at[0], st_sem.at[0]).start()
    pltpu.make_async_copy(rstat, STAT.at[1], st_sem.at[1]).start()

    sub = zl * 2 + c
    z_to = zh * 2 + lax.div(x, 2)
    z_pair = zh * 2 + 1 - zl
    c_to = lax.rem(x, 2)
    mine = pre == x
    not_mine = jnp.logical_not(mine)
    home = lax.div(x, 2) == zl
    away = jnp.logical_not(home)
    passing = x != 2 * (1 - zl) + c

    def rows_of(n, part):
        j = grp if part == 0 else 1 - grp
        return ig_out.at[
            pl.ds(pl.multiple_of(n * 64, 64), 64), pl.ds(pl.multiple_of(j * 512, 512), 512)
        ]

    def result_send(part):
        j = grp if part == 0 else 1 - grp
        OB[part] = ACC[j].reshape(4, 64, 512).astype(jnp.bfloat16)
        rows = rows_of(sub, part)
        for k in (3, 1, 2):
            xt = xs[k]
            dst = dev(xt, y, z, c_to)
            remote(OB.at[part, xt], HOP.at[part, c], (hop_s, (part, k)), hop_r.at[part, c], dst,
                   when=away)
            remote(OB.at[part, xt], rows, (o_s, (part, k)), o_r.at[part, sub], dst, when=home)
        remote(OB.at[part, x], rows, (o_s, (part, 0)), o_r.at[part, sub],
               dev(x, y, z_to, c_to), when=not_mine)

        @pl.when(mine)
        def _():
            cp = pltpu.make_async_copy(OB.at[part, x], rows, loc_sem.at[5])
            cp.start()
            cp.wait()

    def result_pass(part):
        for cc in range(2):
            @pl.when(passing)
            def _():
                arrived(HOP.at[part, cc], hop_r.at[part, cc])

            n = zl * 2 + cc
            remote(HOP.at[part, cc], rows_of(n, part), (hop_s, (part, 4 + cc)), o_r.at[part, n],
                   dev(x, y, z_pair, c), when=passing)

    cot_a(0)
    act_sends()
    cig_sends()

    @pl.when(is_inner)
    def _():
        branch[0] = is_inner
        own(0)
        cot_b(0)
        own(1)
        own(2)
        far(0)
        cot_a(1)
        cot_a(3)
        own(3)
        far(1)
        near(0)
        far(2)
        cot_a(2)
        near(1)
        far(3)
        cot_b(1)
        near(2)
        end(0)
        cot_f(0)
        cot_b(3)
        near(3)
        end(1)
        cot_b(2)
        end(2)
        cot_f(1)
        end(3)
        cot_f(3)
        cot_f(2)
        cig_a()
        own_swap(0)
        own_swap(1)
        own_swap(2)
        own_swap(3)

    @pl.when(is_outer)
    def _():
        branch[0] = is_outer
        own(0)
        cot_b(0)
        own(1)
        own(2)
        cot_a(1)
        cot_a(3)
        own(3)
        near(0)
        near(1)
        far(0)
        cot_a(2)
        near(2)
        far(1)
        near(3)
        cot_b(1)
        far(2)
        end(0)
        cot_f(0)
        cot_b(3)
        far(3)
        end(1)
        cot_b(2)
        end(2)
        cot_f(1)
        end(3)
        cot_f(3)
        cot_f(2)
        cig_a()
        own_swap(0)
        own_swap(1)
        own_swap(2)
        own_swap(3)

    branch[0] = None
    w_first()
    cot_e(0)
    cot_e(1)
    cot_e(3)
    cot_e(2)
    cig_b()
    gradient()
    w_half(1, 0)
    statistic(0, NT, lstat, left_out)
    statistic(1, TN, rstat, right_out)
    root_1(0)
    w_half(1, 1)
    root_2(0)
    root_3(0)
    root_1(1)
    w_half(2, 0)
    cig_f()
    root_2(1)
    root_3(1)
    raw_1()
    raw_2()
    red_start(0)
    red_finish(0)
    red_start(1)
    w_half(2, 1)
    cig_e()
    ig_own()
    red_finish(1)
    red_start(2)
    ig_step(1)
    w_half(3, 0)
    red_finish(2)
    red_start(3)
    ig_step(2)
    w_half(3, 1)
    red_finish(3)
    update()
    ig_step(3)
    result_send(0)
    w_half(4, 0)
    w_half(4, 1)
    result_pass(0)
    ig_step(4)
    result_send(1)
    result_pass(1)

    for q in range(4):
        @pl.when(jnp.logical_not(jnp.logical_and(mine, sub == q)))
        def _():
            for part in range(2):
                arrived(rows_of(q, part), o_r.at[part, q])

    for cp in local_out:
        cp.wait()
    def sent(size, ssem):
        same = RED.at[0] if size == 1024 else WB.at[0, 0, pl.ds(0, size // 512)]
        pltpu.make_async_remote_copy(
            src_ref=same, dst_ref=same, send_sem=ssem[0].at[ssem[1]], recv_sem=o_r.at[0, 0],
            device_id=other, device_id_type=MESH,
        ).wait_send()

    for flag in (None, is_inner, is_outer, not_mine, home, away, passing):
        group = [entry[1:] for entry in sends if entry[0] is flag]

        def drain(group=group):
            for entry in group:
                sent(*entry)

        if flag is None:
            drain()
        else:
            pl.when(flag)(drain)


def whole_call(act, cot, wblk, lstat, rstat):
    any_spec = pl.BlockSpec(memory_space=pl.ANY)
    bf, f32 = jnp.bfloat16, jnp.float32
    square = jax.ShapeDtypeStruct((BLOCK, BLOCK), f32)
    return pl.pallas_call(
        whole_kernel,
        out_shape=(jax.ShapeDtypeStruct((256, 1024), bf), square, square, square),
        in_specs=[any_spec] * 5,
        out_specs=(any_spec,) * 4,
        scratch_shapes=[
            pltpu.VMEM((4, 2, 4, 128, 512), bf),
            pltpu.VMEM((4, 128, 512), bf),
            pltpu.VMEM((4, 2, 4, 2, 64, 512), bf),
            pltpu.VMEM((4, 4, 4, 16, 1024), bf),
            pltpu.VMEM((8, 2, 512, 512), bf),
            pltpu.VMEM((2, 256, 512), f32),
            pltpu.VMEM((2, 4, 64, 512), bf),
            pltpu.VMEM((BLOCK, BLOCK), f32),
            pltpu.VMEM((2, BLOCK, BLOCK), bf),
            pltpu.VMEM((2, BLOCK, BLOCK), f32),
            pltpu.VMEM((BLOCK, BLOCK), f32),
            pltpu.VMEM((BLOCK, BLOCK), f32),
            pltpu.VMEM((2, BLOCK, BLOCK), bf),
            pltpu.VMEM((2, BLOCK, BLOCK), bf),
            pltpu.VMEM((2, 2, BLOCK, BLOCK), bf),
            pltpu.VMEM((BLOCK, BLOCK), f32),
            pltpu.VMEM((19, 8, 128), f32),
            pltpu.VMEM((2, 2, 64, 512), bf),
            DMA((6,)), DMA((4,)), DMA((4,)), DMA((4,)), DMA((4,)),
            DMA((5, 4)), DMA((3, 4)), DMA((4, 4)), DMA((4, 4)),
            DMA((3,)), DMA((3,)), DMA((5, 4)), DMA((5, 4)), DMA((30,)), DMA((30,)),
            DMA((4,)), DMA((4,)), DMA((2, 5, 2)), DMA((2, 5, 2)), DMA((21,)), DMA((21,)),
            DMA((2, 4)), DMA((2, 4)), DMA((15,)), DMA((15,)), DMA((5,)), DMA((2, 6)), DMA((2, 2)),
        ],
        compiler_params=pltpu.CompilerParams(
            collective_id=0, has_side_effects=True, vmem_limit_bytes=60 * 1024 * 1024
        ),
        name="gather_products",
    )(act, cot, wblk, lstat, rstat)


def copy_kernel(*refs):
    n = (len(refs) - 2) // 3
    src, dst, held = refs[:n], refs[n : 2 * n], refs[2 * n : 3 * n]
    into = [pltpu.make_async_copy(src[i], held[i], refs[-2].at[i]) for i in range(n)]
    out = [pltpu.make_async_copy(held[i], dst[i], refs[-1].at[i]) for i in range(n)]
    for cp in into:
        cp.start()
    for i in range(n):
        into[i].wait()
        out[i].start()
    for cp in out:
        cp.wait()


def place(*arrays):
    any_spec = pl.BlockSpec(memory_space=pl.ANY)
    n = len(arrays)
    return pl.pallas_call(
        copy_kernel,
        out_shape=tuple(jax.ShapeDtypeStruct(a.shape, a.dtype) for a in arrays),
        in_specs=[any_spec] * n,
        out_specs=(any_spec,) * n,
        scratch_shapes=[pltpu.VMEM(a.shape, a.dtype) for a in arrays] + [DMA((n,)), DMA((n,))],
        compiler_params=pltpu.CompilerParams(vmem_limit_bytes=60 * 1024 * 1024),
        name="place",
    )(*arrays)


def on_device(activations, cotangent, weight_blocks, left_stat, right_stat):
    square = (BLOCK, BLOCK)
    input_grad, left_next, right_next, update = whole_call(
        activations,
        cotangent,
        weight_blocks.reshape(square),
        left_stat.reshape(square),
        right_stat.reshape(square),
    )
    input_grad, left_next, right_next, update = place(
        input_grad, left_next, right_next, update
    )
    shape_out = left_stat.shape
    return (
        input_grad,
        left_next.reshape(shape_out),
        right_next.reshape(shape_out),
        update.reshape(shape_out),
    )


def solution(mesh):
    block = P("dp", "mp", "pre", None, None)
    return jax.shard_map(
        on_device,
        mesh=mesh,
        in_specs=(P("dp", "mp"), P("dp", "pre"), block, block, block),
        out_specs=(P("dp", ("mp", "pre")), block, block, block),
        check_vma=False,
    )
```

```python
import math

import jax
import jax.numpy as jnp
from jax import lax
from jax.experimental import pallas as pl
from jax.experimental.pallas import tpu as pltpu
from jax.sharding import PartitionSpec as P

D = 4096
FF = 16384
TOKENS = 4096
BLOCK = 512
NX, NY, NZ = 4, 4, 8

DECAY_RATE = 0.9
MESH = pl.DeviceIdType.MESH
DMA = pltpu.SemaphoreType.DMA
C0, C1, C2, C3 = 25 / 16, -(5 + 3125 / 256) / 16, 3125 / 4096, -1250 / 4096
C4, C5, C6 = 250 / 4096, -25 / 4096, 1 / 4096


def split(value):
    high = value.astype(jnp.bfloat16)
    return high, (value - high.astype(jnp.float32)).astype(jnp.bfloat16)


NN = (((1,), (0,)), ((), ()))
NT = (((1,), (1,)), ((), ()))
TN = (((0,), (0,)), ((), ()))


def dot(a, b, dims):
    return lax.dot_general(a, b, dims, preferred_element_type=jnp.float32)


def product(a, b, dims=NN):
    ah, al = a
    bh, bl = b
    return dot(ah, bh, dims) + (dot(ah, bl, dims) + dot(al, bh, dims))


def whole_kernel(
    act, cot, wblk, lstat, rstat,
    ig_out, left_out, right_out, update_out,
    ACT, OUTB, COT, CIG, WB, ACC, OB, G, GS, STAT, T2, T3, MS, CS, PS, RAW, RED, HOP,
    loc_sem, a1_s, a1_r, a1o_s, a1o_r, tz_s, tz_r, sw_s, sw_r,
    b1_s, b1_r, pa_s, pa_r, ring_s, ring_r, c1_s, c1_r, w_s, w_r, ws_s, ws_r, o_s, o_r,
    red_s, red_r, st_sem, hop_s, hop_r,
):
    dp = lax.axis_index("dp")
    y = lax.axis_index("mp")
    pre = lax.axis_index("pre")
    x = lax.div(dp, 4)
    zh = lax.rem(dp, 4)
    zl = lax.div(pre, 2)
    c = lax.rem(pre, 2)
    oc = 1 - c
    z = zh * 2 + zl
    grp = lax.div(z, 4)
    g = lax.rem(z, 4)
    side = lax.div(g, 2)
    inner = lax.rem(lax.div(g + 1, 2), 2)
    d = 1 - 2 * side
    so, sn, sf, se = 1 + side, 3 * side, 2 - side, 3 - 3 * side
    hpar = lax.rem(zh, 2)

    def dev(xx, yy, zz, cc):
        return {
            "dp": xx * 4 + lax.div(zz, 2),
            "mp": yy,
            "pre": lax.rem(zz, 2) * 2 + cc,
        }

    def xp(k):
        return lax.rem(x + k + 4, 4)

    def yp(k):
        return lax.rem(y + k + 4, 4)

    def zp(k):
        return lax.rem(z + k + 8, 8)

    def zp_d(sign):
        return lax.rem(z + sign * d + 8, 8)

    other = dev(x, y, z, oc)

    barrier = pltpu.get_barrier_semaphore()
    count = 0

    def greet(device):
        pl.semaphore_signal(barrier, inc=1, device_id=device, device_id_type=MESH)

    for k in range(1, 4):
        greet({"dp": dp, "mp": y, "pre": lax.rem(pre + k, 4)})
        greet(dev(xp(k), y, z, c))
        greet(dev(xp(k), y, z, oc))
        count += 3
    for k in range(1, 4):
        greet(dev(x, yp(k), z, c))
        count += 1
    pair = lax.rem(z + 1 - 2 * zl + 8, 8)
    for k in range(1, 7):
        greet(dev(x, y, lax.rem(pair + (1 - 2 * zl) * k + 16, 8), c))
        count += 1
    pl.semaphore_wait(barrier, count)

    sends = []
    branch = [None]

    def remote(src, dst, ssem, rsem, device, when=None):
        cp = pltpu.make_async_remote_copy(
            src_ref=src, dst_ref=dst, send_sem=ssem[0].at[ssem[1]], recv_sem=rsem,
            device_id=device, device_id_type=MESH,
        )
        if when is None:
            cp.start()
        else:
            pl.when(when)(cp.start)
        size = math.prod(dst.shape)
        sends.append((branch[0] if when is None else when, size, ssem))

    def arrived(dst, rsem):
        pltpu.make_async_copy(dst, dst, rsem).wait()

    is_inner = inner == 1
    is_outer = inner == 0

    def act_src(xx, gg):
        return act.at[
            pl.ds(pl.multiple_of(c * 128, 128), 128),
            pl.ds(pl.multiple_of(xx * 1024 + gg * 512, 512), 512),
        ]

    rel = (0, -1, 1, 2)
    xs = [xp(r) for r in rel]
    cot_piece = lambda half: cot.at[
        pl.ds(pl.multiple_of(y * 64, 64), 64),
        pl.ds(pl.multiple_of(half * 512, 512), 512),
    ]
    ypair = lax.div(y, 2)
    ylow = lax.rem(y, 2)
    cot_slot = lambda zz: COT.at[zz, ypair, x, ylow]
    pltpu.make_async_copy(cot_piece(hpar), cot_slot(zh), loc_sem.at[0]).start()
    remote(cot_piece(hpar), cot_slot(zh), (b1_s, (0,)), b1_r.at[0], dev(x, y, zp(4), c))
    remote(cot_piece(1 - hpar), cot_slot(zh), (b1_s, (1,)), b1_r.at[1], dev(x, y, zp(2), c))
    remote(cot_piece(1 - hpar), cot_slot(zh), (b1_s, (2,)), b1_r.at[2], dev(x, y, zp(-2), c))
    cig_src = lambda q: cot.at[pl.ds(pl.multiple_of(q * 64 + y * 16, 16), 16), :]

    def cig_sends():
        pltpu.make_async_copy(cig_src(pre), CIG.at[pre, x, y], loc_sem.at[3]).start()
        for k in range(1, 4):
            q = lax.rem(pre + k, 4)
            remote(cig_src(q), CIG.at[pre, x, y], (c1_s, (k,)), c1_r.at[k],
                   {"dp": dp, "mp": y, "pre": q})

    def act_sends():
        pltpu.make_async_copy(act_src(x, grp), ACT.at[so, c, x], loc_sem.at[1]).start()

        @pl.when(is_outer)
        def _():
            pltpu.make_async_copy(act_src(x, 1 - grp), OUTB.at[x], loc_sem.at[2]).start()

        steps = ((1, 1), (2, -1), (3, 2))
        for k, step in steps:
            to = xp(step)
            remote(act_src(to, 1 - grp), OUTB.at[x], (a1o_s, (k,)), a1o_r.at[k],
                   dev(to, y, z, c), when=is_outer)
        for k, step in steps:
            to = xp(step)
            remote(act_src(to, grp), ACT.at[so, c, x], (a1_s, (k,)), a1_r.at[k], dev(to, y, z, c))

    def ring_start(base, unit, my, to_next, to_prev):
        for hf in range(2):
            remote(unit(my, hf), unit(my, hf), (ring_s, (base + hf,)), ring_r.at[base + hf], to_next)
            back = 1 - hf
            remote(unit(my, back), unit(my, back), (ring_s, (base + 2 + back,)),
                   ring_r.at[base + 2 + back], to_prev)

    def ring_forward(base, unit, prv, nxt, to_next, to_prev):
        arrived(unit(prv, 0), ring_r.at[base])
        remote(unit(prv, 0), unit(prv, 0), (ring_s, (base + 4,)), ring_r.at[base + 4], to_next)
        arrived(unit(nxt, 1), ring_r.at[base + 3])
        remote(unit(nxt, 1), unit(nxt, 1), (ring_s, (base + 5,)), ring_r.at[base + 5], to_prev)

    def ring_end(base, unit, prv, nxt, far):
        arrived(unit(prv, 1), ring_r.at[base + 1])
        arrived(unit(nxt, 0), ring_r.at[base + 2])
        arrived(unit(far, 0), ring_r.at[base + 4])
        arrived(unit(far, 1), ring_r.at[base + 5])

    xnext, xprev = dev(xp(1), y, z, c), dev(xp(-1), y, z, c)
    ynext, yprev = dev(x, yp(1), z, c), dev(x, yp(-1), z, c)
    shards = [lax.rem(zh + r, 4) for r in range(4)]

    def cot_unit(r, i, lo):
        if r == 2:
            return COT.at[shards[r], lo, i]
        return COT.at[shards[r], lax.div(i, 2), pl.ds(2 * lo, 2), lax.rem(i, 2)]

    uc = lambda i, lo: CIG.at[pl.ds(2 * lo, 2), :, i]
    xargs = (xp(-1), xp(1), xnext, xprev)
    yargs = (yp(-1), yp(1), ynext, yprev)

    def cot_a(r):
        piece = cot_slot(shards[r])
        if r:
            arrived(piece, b1_r.at[{1: 2, 3: 1, 2: 0}[r]])
        for k in (2, 1, 3):
            to = dev(x, yp(k), z, c) if r == 2 else dev(xp(k), y, z, c)
            remote(piece if r else cot_piece(hpar), piece, (pa_s, (r, k,)), pa_r.at[r, k], to)

    def cot_b(r):
        for k in (1, 3, 2):
            if r == 2:
                arrived(COT.at[shards[r], lax.div(yp(-k), 2), x, lax.rem(yp(-k), 2)], pa_r.at[r, k])
            else:
                arrived(COT.at[shards[r], ypair, xp(-k), ylow], pa_r.at[r, k])
        if r == 0:
            pltpu.make_async_copy(cot_piece(hpar), cot_slot(zh), loc_sem.at[0]).wait()
        unit = lambda i, lo: cot_unit(r, i, lo)
        if r == 2:
            ring_start(6 * r, unit, x, xnext, xprev)
        else:
            ring_start(6 * r, unit, y, ynext, yprev)

    def cot_f(r):
        unit = lambda i, lo: cot_unit(r, i, lo)
        ring_forward(6 * r, unit, *(xargs if r == 2 else yargs))

    def cot_e(r):
        unit = lambda i, lo: cot_unit(r, i, lo)
        m = xp if r == 2 else yp
        ring_end(6 * r, unit, m(-1), m(1), m(2))

    def cig_a():
        pltpu.make_async_copy(cig_src(pre), CIG.at[pre, x, y], loc_sem.at[3]).wait()
        for k in range(1, 4):
            arrived(CIG.at[lax.rem(pre + 4 - k, 4), x, y], c1_r.at[k])
        for k in (2, 1, 3):
            piece = CIG.at[:, x, y]
            remote(piece, piece, (pa_s, (4, k)), pa_r.at[4, k], dev(xp(k), y, z, c))

    def cig_b():
        for k in (1, 3, 2):
            arrived(CIG.at[:, xp(-k), y], pa_r.at[4, k])
        ring_start(24, uc, y, ynext, yprev)

    def cig_f():
        ring_forward(24, uc, *yargs)

    def cig_e():
        ring_end(24, uc, yp(-1), yp(1), yp(2))

    inward = dev(x, y, zp_d(1), c)
    outward = dev(x, y, zp_d(-1), c)

    def swap(kind, k, slot):
        piece = ACT.at[slot, c, xs[k]]
        remote(piece, piece, (sw_s, (kind, k,)), sw_r.at[kind, k], other)

    def own(k):
        piece = ACT.at[so, c, xs[k]]
        if branch[0] is is_outer:
            if k == 0:
                pltpu.make_async_copy(act_src(x, 1 - grp), OUTB.at[x], loc_sem.at[2]).wait()
            else:
                arrived(OUTB.at[xs[k]], a1o_r.at[k])
            remote(OUTB.at[xs[k]], ACT.at[3 - sn, c, xs[k]],
                   (tz_s, (0, k,)), tz_r.at[0, k], outward)
        else:
            own_here(k, piece)
            remote(piece, piece, (tz_s, (1, k,)), tz_r.at[1, k], inward)

    def own_here(k, piece):
        if k == 0:
            pltpu.make_async_copy(act_src(x, grp), piece, loc_sem.at[1]).wait()
        else:
            arrived(piece, a1_r.at[k])

    def own_swap(k):
        piece = ACT.at[so, c, xs[k]]
        if branch[0] is is_outer:
            own_here(k, piece)
        swap(3, k, so)

    def near(k):
        piece = ACT.at[sn, c, xs[k]]
        arrived(piece, tz_r.at[0, k])
        remote(piece, piece, (tz_s, (2, k,)),
               tz_r.at[0 if branch[0] is is_outer else 2, k], inward)
        swap(0, k, sn)

    def far(k):
        piece = ACT.at[sf, c, xs[k]]
        arrived(piece, tz_r.at[1, k])
        if branch[0] is is_inner:
            remote(piece, piece, (tz_s, (3, k,)), tz_r.at[1, k], outward)
        swap(1, k, sf)

    def end(k):
        piece = ACT.at[se, c, xs[k]]
        arrived(piece, tz_r.at[2, k])
        if branch[0] is is_inner:
            remote(piece, piece, (tz_s, (4, k,)), tz_r.at[2, k], outward)
        swap(2, k, se)

    znext, zprev = dev(x, y, zp(1), c), dev(x, y, zp(-1), c)
    wpart = lambda zz, hf: WB.at[zz, c, pl.ds(hf * 256, 256)]

    def w_send(way, t, hf):
        zz = zp(-(t - 1)) if way == 0 else zp(t - 1)
        remote(wblk.at[pl.ds(hf * 256, 256)] if t == 1 else wpart(zz, hf), wpart(zz, hf),
               (w_s, (way, t, hf,)), w_r.at[way, t, hf], znext if way == 0 else zprev)

    def w_index(way, t, hf):
        return 1 + (way * 5 + t) * 2 + hf

    def w_arrive(way, t, hf):
        zz = zp(-t) if way == 0 else zp(t)
        arrived(wpart(zz, hf), w_r.at[way, t, hf])
        if t < 3 or (t == 3 and hf == way):
            w_send(way, t + 1, hf)
        n = w_index(way, t, hf)
        remote(wpart(zz, hf), wpart(zz, hf), (ws_s, (n,)), ws_r.at[n], other)

    def w_first():
        pltpu.make_async_copy(wblk, WB.at[z, c], loc_sem.at[4]).start()
        remote(wblk, WB.at[z, c], (ws_s, (0,)), ws_r.at[0], other)
        for hf in range(2):
            for way in range(2):
                w_send(way, 1, hf)

    def w_half(t, hf):
        for way in range(2):
            if t < 4 or hf == way:
                w_arrive(way, t, hf)

    def ig_chip(zz):
        for cc in range(2):
            p = lax.rem(zz, 2) * 2 + cc
            h = lax.rem(lax.div(zz, 2), 2)
            a = CIG[p, :, :, :, pl.ds(pl.multiple_of(h * 512, 512), 512)].reshape(256, 512)
            ACC[lax.div(zz, 4)] += dot(a, WB[zz, cc], NT)

    def ig_own():
        pltpu.make_async_copy(wblk, WB.at[z, c], loc_sem.at[4]).wait()
        arrived(WB.at[z, oc], ws_r.at[0])
        ACC[...] = jnp.zeros_like(ACC)
        ig_chip(z)

    def ig_wait(way, t):
        zz = zp(-t) if way == 0 else zp(t)
        for hf in range(2):
            if t < 4 or hf == way:
                arrived(WB.at[zz, oc, pl.ds(hf * 256, 256)], ws_r.at[w_index(way, t, hf)])

    def ig_step(t):
        for way in range(2):
            ig_wait(way, t)
            if t < 4:
                ig_chip(zp(-t) if way == 0 else zp(t))
        if t == 4:
            ig_chip(zp(4))

    def gradient():
        for kind, slot in ((3, so), (0, sn), (1, sf), (2, se)):
            for k in range(4):
                arrived(ACT.at[slot, oc, xs[k]], sw_r.at[kind, k])
        G[...] = jnp.zeros_like(G)

        @pl.loop(0, 8)
        def _(i):
            s = lax.div(i, 2)
            cc = lax.rem(i, 2)
            shard = lax.rem(2 * grp + 3 + s, 4)
            a = ACT[s, cc].reshape(BLOCK, BLOCK)
            b = COT[shard, cc].reshape(BLOCK, BLOCK)
            G[...] += dot(a, b, TN)

        grad = G[...] * (1.0 / TOKENS)
        high, low = split(grad)
        GS[0] = high
        GS[1] = low

    pair_of = lambda ref: (ref[0], ref[1])

    def put(ref, value):
        high, low = split(value)
        ref[0] = high
        ref[1] = low

    def statistic(i, dims, old, new):
        pltpu.make_async_copy(old, STAT.at[i], st_sem.at[i]).wait()
        g = pair_of(GS)
        STAT[i] = DECAY_RATE * STAT[i] + (1.0 - DECAY_RATE) * product(g, g, dims)
        cp = pltpu.make_async_copy(STAT.at[i], new, st_sem.at[2 + i])
        cp.start()
        local_out.append(cp)

    scale = [None, None]

    def root_1(i):
        a = STAT[i]
        z_of = 2.5 * lax.rsqrt(jnp.sum(a * a, axis=(0, 1), keepdims=True))
        scale[i] = z_of
        put(MS, z_of * a)
        T2[...] = product(pair_of(MS), pair_of(MS))
        put(CS, T2[...])

    def root_2(i):
        T3[...] = product(pair_of(MS), pair_of(CS))

    def root_3(i):
        m = scale[i] * STAT[i]
        put(CS, C4 * m + C5 * T2[...] + C6 * T3[...])
        put(MS, T3[...])
        eye = (
            lax.broadcasted_iota(jnp.int32, (BLOCK, BLOCK), 0)
            == lax.broadcasted_iota(jnp.int32, (BLOCK, BLOCK), 1)
        )
        low_part = C1 * m + C2 * T2[...] + C3 * T3[...] + jnp.where(eye, C0, 0.0)
        whole = low_part + product(pair_of(MS), pair_of(CS))
        put(PS.at[i], jnp.sqrt(jnp.sqrt(scale[i])) * whole)

    def raw_1():
        put(CS, product(pair_of(PS.at[0]), pair_of(GS)))

    def raw_2():
        raw = product(pair_of(CS), pair_of(PS.at[1]))
        RAW[...] = raw
        RED[0] = jnp.broadcast_to(jnp.sum(raw * raw, axis=(0, 1), keepdims=True), (8, 128))

    def red_targets(stage):
        if stage == 0:
            return [(1, other)]
        if stage == 1:
            return [(1 + k, dev(x, y, zp(k), c)) for k in range(1, 8)]
        if stage == 2:
            return [(8 + k, dev(xp(k), y, z, c)) for k in range(1, 4)]
        return [(11 + k, dev(x, yp(k), z, c)) for k in range(1, 4)]

    def red_send(stage):
        for slot, device in red_targets(stage):
            remote(RED.at[15 + stage], RED.at[slot], (red_s, (slot,)), red_r.at[slot], device)

    def red_start(stage):
        RED[15 + stage] = RED[0]
        red_send(stage)

    def red_finish(stage):
        total = RED[0]
        for slot, _ in red_targets(stage):
            arrived(RED.at[slot], red_r.at[slot])
            total = total + RED[slot]
        RED[0] = total

    def update():
        mean_square = RED[0, 0:1, 0:1] * (1.0 / (FF * D))
        RAW[...] = RAW[...] * lax.rsqrt(mean_square + 1e-06)
        cp = pltpu.make_async_copy(RAW, update_out, st_sem.at[4])
        cp.start()
        local_out.append(cp)

    local_out = []
    pltpu.make_async_copy(lstat, STAT.at[0], st_sem.at[0]).start()
    pltpu.make_async_copy(rstat, STAT.at[1], st_sem.at[1]).start()

    sub = zl * 2 + c
    z_to = zh * 2 + lax.div(x, 2)
    z_pair = zh * 2 + 1 - zl
    c_to = lax.rem(x, 2)
    mine = pre == x
    not_mine = jnp.logical_not(mine)
    home = lax.div(x, 2) == zl
    away = jnp.logical_not(home)
    passing = x != 2 * (1 - zl) + c

    def rows_of(n, part):
        j = grp if part == 0 else 1 - grp
        return ig_out.at[
            pl.ds(pl.multiple_of(n * 64, 64), 64), pl.ds(pl.multiple_of(j * 512, 512), 512)
        ]

    def result_send(part):
        j = grp if part == 0 else 1 - grp
        OB[part] = ACC[j].reshape(4, 64, 512).astype(jnp.bfloat16)
        rows = rows_of(sub, part)
        for k in (3, 1, 2):
            xt = xs[k]
            dst = dev(xt, y, z, c_to)
            remote(OB.at[part, xt], HOP.at[part, c], (hop_s, (part, k)), hop_r.at[part, c], dst,
                   when=away)
            remote(OB.at[part, xt], rows, (o_s, (part, k)), o_r.at[part, sub], dst, when=home)
        remote(OB.at[part, x], rows, (o_s, (part, 0)), o_r.at[part, sub],
               dev(x, y, z_to, c_to), when=not_mine)

        @pl.when(mine)
        def _():
            cp = pltpu.make_async_copy(OB.at[part, x], rows, loc_sem.at[5])
            cp.start()
            cp.wait()

    def result_pass(part):
        for cc in range(2):
            @pl.when(passing)
            def _():
                arrived(HOP.at[part, cc], hop_r.at[part, cc])

            n = zl * 2 + cc
            remote(HOP.at[part, cc], rows_of(n, part), (hop_s, (part, 4 + cc)), o_r.at[part, n],
                   dev(x, y, z_pair, c), when=passing)

    cot_a(0)
    act_sends()
    cig_sends()

    @pl.when(is_inner)
    def _():
        branch[0] = is_inner
        own(0)
        cot_b(0)
        own(1)
        own(2)
        far(0)
        cot_a(1)
        cot_a(3)
        own(3)
        far(1)
        near(0)
        far(2)
        cot_a(2)
        near(1)
        far(3)
        cot_b(1)
        near(2)
        end(0)
        cot_f(0)
        cot_b(3)
        near(3)
        end(1)
        cot_b(2)
        end(2)
        cot_f(1)
        end(3)
        cot_f(3)
        cot_f(2)
        cig_a()
        own_swap(0)
        own_swap(1)
        own_swap(2)
        own_swap(3)

    @pl.when(is_outer)
    def _():
        branch[0] = is_outer
        own(0)
        cot_b(0)
        own(1)
        own(2)
        cot_a(1)
        cot_a(3)
        own(3)
        near(0)
        near(1)
        far(0)
        cot_a(2)
        near(2)
        far(1)
        near(3)
        cot_b(1)
        far(2)
        end(0)
        cot_f(0)
        cot_b(3)
        far(3)
        end(1)
        cot_b(2)
        end(2)
        cot_f(1)
        end(3)
        cot_f(3)
        cot_f(2)
        cig_a()
        own_swap(0)
        own_swap(1)
        own_swap(2)
        own_swap(3)

    branch[0] = None
    w_first()
    cot_e(0)
    cot_e(1)
    cot_e(3)
    cot_e(2)
    cig_b()
    gradient()
    w_half(1, 0)
    statistic(0, NT, lstat, left_out)
    statistic(1, TN, rstat, right_out)
    root_1(0)
    w_half(1, 1)
    root_2(0)
    root_3(0)
    root_1(1)
    w_half(2, 0)
    cig_f()
    root_2(1)
    root_3(1)
    raw_1()
    raw_2()
    red_start(0)
    red_finish(0)
    red_start(1)
    w_half(2, 1)
    cig_e()
    ig_own()
    red_finish(1)
    red_start(2)
    ig_step(1)
    w_half(3, 0)
    red_finish(2)
    red_start(3)
    ig_step(2)
    w_half(3, 1)
    ig_step(3)
    result_send(0)
    red_finish(3)
    update()
    w_half(4, 0)
    w_half(4, 1)
    result_pass(0)
    ig_step(4)
    result_send(1)
    result_pass(1)

    for q in range(4):
        @pl.when(jnp.logical_not(jnp.logical_and(mine, sub == q)))
        def _():
            for part in range(2):
                arrived(rows_of(q, part), o_r.at[part, q])

    for cp in local_out:
        cp.wait()
    def sent(size, ssem):
        same = RED.at[0] if size == 1024 else WB.at[0, 0, pl.ds(0, size // 512)]
        pltpu.make_async_remote_copy(
            src_ref=same, dst_ref=same, send_sem=ssem[0].at[ssem[1]], recv_sem=o_r.at[0, 0],
            device_id=other, device_id_type=MESH,
        ).wait_send()

    for flag in (None, is_inner, is_outer, not_mine, home, away, passing):
        group = [entry[1:] for entry in sends if entry[0] is flag]

        def drain(group=group):
            for entry in group:
                sent(*entry)

        if flag is None:
            drain()
        else:
            pl.when(flag)(drain)


def whole_call(act, cot, wblk, lstat, rstat):
    any_spec = pl.BlockSpec(memory_space=pl.ANY)
    bf, f32 = jnp.bfloat16, jnp.float32
    square = jax.ShapeDtypeStruct((BLOCK, BLOCK), f32)
    return pl.pallas_call(
        whole_kernel,
        out_shape=(jax.ShapeDtypeStruct((256, 1024), bf), square, square, square),
        in_specs=[any_spec] * 5,
        out_specs=(any_spec,) * 4,
        scratch_shapes=[
            pltpu.VMEM((4, 2, 4, 128, 512), bf),
            pltpu.VMEM((4, 128, 512), bf),
            pltpu.VMEM((4, 2, 4, 2, 64, 512), bf),
            pltpu.VMEM((4, 4, 4, 16, 1024), bf),
            pltpu.VMEM((8, 2, 512, 512), bf),
            pltpu.VMEM((2, 256, 512), f32),
            pltpu.VMEM((2, 4, 64, 512), bf),
            pltpu.VMEM((BLOCK, BLOCK), f32),
            pltpu.VMEM((2, BLOCK, BLOCK), bf),
            pltpu.VMEM((2, BLOCK, BLOCK), f32),
            pltpu.VMEM((BLOCK, BLOCK), f32),
            pltpu.VMEM((BLOCK, BLOCK), f32),
            pltpu.VMEM((2, BLOCK, BLOCK), bf),
            pltpu.VMEM((2, BLOCK, BLOCK), bf),
            pltpu.VMEM((2, 2, BLOCK, BLOCK), bf),
            pltpu.VMEM((BLOCK, BLOCK), f32),
            pltpu.VMEM((19, 8, 128), f32),
            pltpu.VMEM((2, 2, 64, 512), bf),
            DMA((6,)), DMA((4,)), DMA((4,)), DMA((4,)), DMA((4,)),
            DMA((5, 4)), DMA((3, 4)), DMA((4, 4)), DMA((4, 4)),
            DMA((3,)), DMA((3,)), DMA((5, 4)), DMA((5, 4)), DMA((30,)), DMA((30,)),
            DMA((4,)), DMA((4,)), DMA((2, 5, 2)), DMA((2, 5, 2)), DMA((21,)), DMA((21,)),
            DMA((2, 4)), DMA((2, 4)), DMA((15,)), DMA((15,)), DMA((5,)), DMA((2, 6)), DMA((2, 2)),
        ],
        compiler_params=pltpu.CompilerParams(
            collective_id=0, has_side_effects=True, vmem_limit_bytes=60 * 1024 * 1024
        ),
        name="gather_products",
    )(act, cot, wblk, lstat, rstat)


def copy_kernel(*refs):
    n = (len(refs) - 2) // 3
    src, dst, held = refs[:n], refs[n : 2 * n], refs[2 * n : 3 * n]
    into = [pltpu.make_async_copy(src[i], held[i], refs[-2].at[i]) for i in range(n)]
    out = [pltpu.make_async_copy(held[i], dst[i], refs[-1].at[i]) for i in range(n)]
    for cp in into:
        cp.start()
    for i in range(n):
        into[i].wait()
        out[i].start()
    for cp in out:
        cp.wait()


def place(*arrays):
    any_spec = pl.BlockSpec(memory_space=pl.ANY)
    n = len(arrays)
    return pl.pallas_call(
        copy_kernel,
        out_shape=tuple(jax.ShapeDtypeStruct(a.shape, a.dtype) for a in arrays),
        in_specs=[any_spec] * n,
        out_specs=(any_spec,) * n,
        scratch_shapes=[pltpu.VMEM(a.shape, a.dtype) for a in arrays] + [DMA((n,)), DMA((n,))],
        compiler_params=pltpu.CompilerParams(vmem_limit_bytes=60 * 1024 * 1024),
        name="place",
    )(*arrays)


def on_device(activations, cotangent, weight_blocks, left_stat, right_stat):
    square = (BLOCK, BLOCK)
    input_grad, left_next, right_next, update = whole_call(
        activations,
        cotangent,
        weight_blocks.reshape(square),
        left_stat.reshape(square),
        right_stat.reshape(square),
    )
    input_grad, left_next, right_next, update = place(
        input_grad, left_next, right_next, update
    )
    shape_out = left_stat.shape
    return (
        input_grad,
        left_next.reshape(shape_out),
        right_next.reshape(shape_out),
        update.reshape(shape_out),
    )


def solution(mesh):
    block = P("dp", "mp", "pre", None, None)
    return jax.shard_map(
        on_device,
        mesh=mesh,
        in_specs=(P("dp", "mp"), P("dp", "pre"), block, block, block),
        out_specs=(P("dp", ("mp", "pre")), block, block, block),
        check_vma=False,
    )
```
